512 devices in a mesh: dp: 128 (over z, y, core), mp: 4 (over x).
Axes of the slice: x: 4, y: 8, z: 8, core: 2. Of those that a mesh axis runs over, the one named last changes fastest.
Arguments:
- images: bfloat16 [32768, 1664], P('dp'), may hold values from -6 to 6
- attn_gain: float32 [1664], replicated, may hold values from 0.25 to 1.75
- qkv_weight: bfloat16 [3, 1664, 1664], P(None, 'dp', 'mp'), may hold values from -12 to 12
- proj_weight: bfloat16 [1664, 1664], P('mp', 'dp'), may hold values from -0.15625 to 0.15625
- mlp_gain: float32 [1664], replicated, may hold values from 0.25 to 1.75
- expert_in: bfloat16 [1664, 262144], P(None, ('dp', 'mp')), may hold values from -0.15625 to 0.15625
- expert_out: bfloat16 [262144, 1664], P(('dp', 'mp')), may hold values from -0.0625 to 0.0625
- gate_values: bfloat16 [32768, 2], P('dp'), may hold values from 0.25 to 1, as said below
- expert_ids: int32 [32768, 2], P('dp'), may hold values from 0 to 31, as said below
- kept_patches: int32 [128, 32, 8], P('dp'), may hold values from 0 to 255, as said below
- kept_counts: int32 [128, 32], P('dp'), may hold values from 0 to 8, as said below
Outputs:
- block_out: bfloat16 [32768, 1664], P(('dp', 'mp'))
The draws below stay inside these ranges and needn't reach their ends.
Inputs may be any that keep to these rules, and one draw needn't show every extreme that they name: `expert_ids`: each token names 2 different experts. `kept_patches`: for image i and expert e, slots 0 to kept_counts[i, e] - 1 hold different patches of image i whose expert_ids name e, in order of priority: patches ordered by their largest gate value, larger first, ties by lower patch number; every patch naming e that is not listed there has lower priority than all listed ones and was dropped because those slots are full; the later slots are padding with patch numbers of that image. `kept_counts`: the number of valid slots; it equals 8 wherever 8 or more patches of the image name the expert, else the number of such patches. `gate_values`: each patch's first gate value is larger than its second.
All inputs are finite; a program needn't handle non-finite values.
Results may differ from the reference program's by a relative error of at most 0.015.
Values may be sent and summed in bfloat16 or wider, within the bound.
A program may use at most 64 MiB of HBM per device.

```python
import jax
import jax.numpy as jnp
from jax import lax

D = 1664
HEADS = 16
FF = 8192
EXPERTS = 32
PATCHES = 256
HEAD_DIM = 104
CAP = 8
IMAGES = 128
TOKENS = 32768
GROUP = 16
SLICE = 512


def routing_tables(key):
    subkeys = jax.random.split(key, 5)
    labels = jax.random.permutation(subkeys[0], EXPERTS)
    first_low = jnp.minimum(jax.random.randint(subkeys[1], (IMAGES, PATCHES), 0, EXPERTS), jax.random.randint(subkeys[2], (IMAGES, PATCHES), 0, EXPERTS))
    first_id = jnp.take(labels, first_low)
    second = (first_id + 1 + jax.random.randint(subkeys[3], (IMAGES, PATCHES), 0, EXPERTS - 1)) % EXPERTS
    chosen_ids = jnp.stack([first_id, second], axis=-1)
    level_keys = jax.random.split(subkeys[4], 2)
    first_level = jax.random.randint(level_keys[0], (IMAGES, PATCHES), 0, 128)
    second_level = jax.random.randint(level_keys[1], (IMAGES, PATCHES), 0, 128)
    gates = jnp.stack([0.5 + first_level.astype(jnp.float32) / 256.0, 0.25 + second_level.astype(jnp.float32) / 512.0], axis=-1)
    score = (127 - first_level) * PATCHES + jnp.arange(PATCHES, dtype=jnp.int32)[None, :]
    ordering_all = jnp.argsort(score, axis=-1)
    priority = jnp.argsort(ordering_all, axis=-1)
    member = jnp.any(chosen_ids[:, :, None, :] == jnp.arange(EXPERTS)[None, None, :, None], axis=-1)
    ranked = jnp.where(member, priority[:, :, None], PATCHES + priority[:, :, None])
    ordering = jnp.argsort(jnp.transpose(ranked, (0, 2, 1)), axis=-1)[:, :, :CAP]
    counts = jnp.minimum(jnp.sum(member.astype(jnp.int32), axis=1), CAP)
    padded = jnp.where(jnp.arange(CAP)[None, None, :] < counts[:, :, None], ordering, ordering[:, :, :1])
    return (chosen_ids.reshape(IMAGES * PATCHES, 2).astype(jnp.int32), padded.astype(jnp.int32), counts.astype(jnp.int32), gates.reshape(IMAGES * PATCHES, 2))


def draw_expert_ids(key, part):
    tables = routing_tables(key)
    return tables[0]


def draw_kept_patches(key, part):
    tables = routing_tables(key)
    return tables[1]


def draw_kept_counts(key, part):
    tables = routing_tables(key)
    return tables[2]


def draw_gate_values(key, part):
    tables = routing_tables(key)
    return tables[3].astype(jnp.bfloat16)


def draw_qkv_weight(key, part):
    key = jax.random.fold_in(key, 11)
    base = jnp.clip(jax.random.normal(key, (3, D, D), jnp.float32), -5.0, 5.0) * D ** (-0.5)
    return base.astype(jnp.bfloat16)


def block_scale(stream_key, extent, cuts, low, high):
    level, own = 1.0, jax.random.fold_in(stream_key, 6)
    for dim, parts in cuts:
        steps = jnp.exp(jax.random.uniform(jax.random.fold_in(own, dim), (parts,), jnp.float32, low / len(cuts), high / len(cuts)))
        level = level * jnp.repeat(steps, extent[dim] // parts).reshape([-1 if axis == dim else 1 for axis in range(len(extent))])
    return level


def scatter_about(own_key, extent, deviation, most, cuts=(), kind=jnp.bfloat16):
    drawn = deviation * jax.random.normal(own_key, extent, jnp.float32)
    if cuts:
        drawn = drawn * block_scale(own_key, extent, cuts, -0.22, 0.18)
    return jnp.clip(drawn, -most, most).astype(kind)


def setup_inputs(seed: int = 0) -> dict:
    seeds = jax.random.split(jax.random.key(seed), 12)
    images = scatter_about(seeds[0], (TOKENS, D), 1.0, 6.0, ((0, 128),))
    attn_gain = jnp.clip(1.0 + 0.15 * jax.random.normal(seeds[1], (D,), jnp.float32), 0.25, 1.75)
    qkv_weight = draw_qkv_weight(jax.random.fold_in(seeds[11], 71), 0)
    proj_weight = scatter_about(seeds[3], (D, D), D ** -0.5, 0.15625, ((0, 4), (1, 128)))
    mlp_gain = jnp.clip(1.0 + 0.15 * jax.random.normal(seeds[4], (D,), jnp.float32), 0.25, 1.75)
    expert_in = scatter_about(seeds[5], (D, EXPERTS * FF), D ** -0.5, 0.15625, ((1, 512),))
    expert_out = scatter_about(seeds[6], (EXPERTS * FF, D), FF ** -0.5, 0.0625, ((0, 512),))
    gate_values = draw_gate_values(jax.random.fold_in(seeds[11], 71), 0)
    expert_ids = draw_expert_ids(jax.random.fold_in(seeds[11], 71), 0)
    kept_patches = draw_kept_patches(jax.random.fold_in(seeds[11], 71), 0)
    kept_counts = draw_kept_counts(jax.random.fold_in(seeds[11], 71), 0)
    return dict(images=images, attn_gain=attn_gain, qkv_weight=qkv_weight, proj_weight=proj_weight, mlp_gain=mlp_gain, expert_in=expert_in, expert_out=expert_out, gate_values=gate_values, expert_ids=expert_ids, kept_patches=kept_patches, kept_counts=kept_counts)


def layer_norm(values, norm_gain):
    center = values - lax.optimization_barrier(jnp.mean(values, axis=-1, keepdims=True))
    spread = lax.optimization_barrier(jnp.mean(center * center, axis=-1, keepdims=True))
    return center * lax.rsqrt(spread + 1e-06) * norm_gain.astype(jnp.float32)

def gelu_tanh(values):
    return 0.5 * values * (1.0 + jnp.tanh(0.7978845608028654 * (values + 0.044715 * values * values * values)))

def reference(images, attn_gain, qkv_weight, proj_weight, mlp_gain, expert_in, expert_out, gate_values, expert_ids, kept_patches, kept_counts):
    inputs = images.astype(jnp.float32)
    normed = layer_norm(inputs, attn_gain).astype(jnp.bfloat16)
    query_rows = jnp.dot(normed, qkv_weight[0], preferred_element_type=jnp.float32).astype(jnp.bfloat16)
    key_rows = jnp.dot(normed, qkv_weight[1], preferred_element_type=jnp.float32).astype(jnp.bfloat16)
    value_rows = jnp.dot(normed, qkv_weight[2], preferred_element_type=jnp.float32).astype(jnp.bfloat16)

    def shaped(block):
        return block.reshape(PATCHES, HEADS, HEAD_DIM).astype(jnp.float32)

    def attend(blocks):
        query_img, key_img, value_img = blocks
        scores = jnp.einsum('phd,qhd->hpq', shaped(query_img), shaped(key_img)) * HEAD_DIM ** (-0.5)
        probs = jax.nn.softmax(scores, axis=-1).astype(jnp.bfloat16)
        mixed = jnp.einsum('hpq,qhd->phd', probs.astype(jnp.float32), shaped(value_img))
        return mixed.astype(jnp.bfloat16).reshape(PATCHES, D)
    heads_out = lax.map(attend, (query_rows.reshape(IMAGES, PATCHES, D), key_rows.reshape(IMAGES, PATCHES, D), value_rows.reshape(IMAGES, PATCHES, D))).reshape(TOKENS, D)
    residual = inputs + jnp.dot(heads_out, proj_weight, preferred_element_type=jnp.float32)
    routed = layer_norm(residual, mlp_gain).astype(jnp.bfloat16)
    token_base = (jnp.arange(IMAGES, dtype=jnp.int32) * PATCHES)[:, None]
    slot_index = jnp.arange(CAP, dtype=jnp.int32)[None, :]

    def one_expert(running, expert):
        token_rows = (kept_patches[:, expert, :] + token_base).reshape(-1).astype(jnp.int32)
        usable = (slot_index < kept_counts[:, expert][:, None]).reshape(-1)
        chosen = jnp.take(routed, token_rows, axis=0)
        in_cols = lax.dynamic_slice_in_dim(expert_in, (expert * FF).astype(jnp.int32), FF, 1)
        hidden = gelu_tanh(jnp.dot(chosen, in_cols, preferred_element_type=jnp.float32)).astype(jnp.bfloat16)
        out_rows = lax.dynamic_slice_in_dim(expert_out, (expert * FF).astype(jnp.int32), FF, 0).reshape(GROUP, SLICE, D)
        partial_value = jnp.einsum('rgs,gsd->grd', hidden.reshape(-1, GROUP, SLICE).astype(jnp.float32), out_rows.astype(jnp.float32)).astype(jnp.bfloat16)
        combined = lax.optimization_barrier(jnp.sum(partial_value.astype(jnp.float32), axis=0))
        matching = jnp.take(expert_ids, token_rows, axis=0) == expert
        weight = lax.optimization_barrier(jnp.sum(jnp.where(matching, jnp.take(gate_values, token_rows, axis=0).astype(jnp.float32), jnp.float32(0.0)), axis=1))
        weight = jnp.where(usable, weight, jnp.float32(0.0))
        return (running.at[token_rows].add(weight[:, None] * combined), None)
    expert_total, _ = lax.scan(one_expert, jnp.zeros((TOKENS, D), jnp.float32), jnp.arange(EXPERTS, dtype=jnp.int32))
    return (residual + expert_total).astype(jnp.bfloat16)
```

```python
import functools

import jax
import jax.numpy as jnp
from jax import lax
from jax.experimental import pallas as pl
from jax.experimental.pallas import tpu as pltpu
from jax.sharding import PartitionSpec as P

MESH = pl.DeviceIdType.MESH
EXPERTS = 32
PATCHES = 256
HEAD_DIM = 104
HEADS_HERE = 4
D = 1664
NX, NY, NZ = 4, 8, 8
STRIP = 13
ROWS = 16
QW = 384
QP = 512
F32 = jnp.float32
BF16 = jnp.bfloat16


def place():
    dp = lax.axis_index("dp")
    return lax.axis_index("mp"), (dp // 2) % NY, dp // (2 * NY), dp % 2


def device(x, y, z, c):
    return ((z * NY + y) * 2 + c, x)


def remote(src, dst, send, recv, target):
    return pltpu.make_async_remote_copy(
        src_ref=src, dst_ref=dst, send_sem=send, recv_sem=recv, device_id=target, device_id_type=MESH
    )


def greet(partners):
    barrier = pltpu.get_barrier_semaphore()
    for partner in partners:
        pl.semaphore_signal(barrier, inc=1, device_id=partner, device_id_type=MESH)
    pl.semaphore_wait(barrier, len(partners))


def strip_pick(feature0, rows, chunk, cols):
    feature = lax.broadcasted_iota(jnp.int32, (rows, cols), 0) + feature0
    col = lax.broadcasted_iota(jnp.int32, (rows, cols), 1)
    inner = col & (ROWS - 1)
    hit = (feature == chunk * 208 + STRIP * (col >> 4) + inner) & (inner < STRIP)
    return jnp.where(hit, 1.0, 0.0).astype(BF16)


def dot(a, b, dims=((1,), (0,))):
    return lax.dot_general(a, b, (dims, ((), ())), preferred_element_type=F32)


HALVES = ((0, 896), (896, 768))


def attention_kernel(
    images, attn_gain, mlp_gain, strips, residual_out, routed_out,
    wg, expanded, acc, outp, summed, landed, stats, stats_in,
    s1_send, s1_recv, ring_send, ring_recv, core_send, core_recv, x_send, x_recv, t_send, t_recv, st_send, st_recv,
):
    x, y, z, c = place()

    def xdev(d):
        return device((x + d) % NX, y, z, c)

    def ydev(d):
        return device(x, (y + d) % NY, z, c)

    def zdev(d):
        return device(x, y, (z + d) % NZ, c)

    core = device(x, y, z, 1 - c)

    @pl.when(x != 0)
    def _():
        landed[:, :, QW:QP] = jnp.zeros((3, PATCHES, QP - QW), BF16)

    wg[z, y, c] = strips[...]
    greet([xdev(d) for d in (1, 2, 3)] + [ydev(d) for d in range(1, NY)] + [zdev(d) for d in range(1, NZ)] + [core])

    first = []
    for half, (lane, width) in enumerate(HALVES):
        for d in range(1, 8):
            target = zdev(d) if half == 0 else ydev(d)
            piece = wg.at[z, y, c, :, lane : lane + width]
            copy = remote(piece, piece, s1_send.at[half, d - 1], s1_recv.at[half, d - 1], target)
            copy.start()
            first.append(copy)

    values = images[...].astype(F32)
    center = values - jnp.mean(values, axis=-1, keepdims=True)
    spread = jnp.mean(center * center, axis=-1, keepdims=True)
    normed = (center * lax.rsqrt(spread + 1e-06) * attn_gain[...]).astype(BF16)
    for m in range(8):
        low = (208 * m) // 128 * 128
        wide = min(384, D - low)
        expanded[m] = dot(normed[:, low : low + wide], strip_pick(low, wide, m, 256)).astype(BF16)

    for copy in first:
        copy.wait()

    def block(half, pos, part):
        lane, width = HALVES[half]
        if half == 0:
            return wg.at[pl.ds(4 * part, 4), pos % NY, c, :, lane : lane + width]
        return wg.at[pos % NZ, pl.ds(4 * part, 4), c, :, lane : lane + width]

    def here(half):
        return y if half == 0 else z

    def ring_copy(half, way, step, part):
        pos = here(half) - (step - 1) if way == 0 else here(half) + (step - 1)
        piece = block(half, pos + 8, part)
        sign = 1 if way == 0 else -1
        target = ydev(8 + sign) if half == 0 else zdev(8 + sign)
        index = (step - 1) * 2 + part
        return remote(piece, piece, ring_send.at[half, way, index], ring_recv.at[half, way, index], target)

    def core_copy(half, slot, pos, part):
        piece = block(half, pos + 8, part)
        return remote(piece, piece, core_send.at[half, slot], core_recv.at[half, slot], core)

    started = []
    for part in range(2):
        for half in range(2):
            for way in range(2):
                copy = ring_copy(half, way, 1, part)
                copy.start()
                started.append(copy)
    for part in range(2):
        for half in range(2):
            copy = core_copy(half, part, here(half), part)
            copy.start()
            started.append(copy)
    slot = 2
    for step in range(1, 5):
        for part in range(2):
            for way in range(2):
                if step == 4 and part != way:
                    continue
                for half in range(2):
                    ring_copy(half, way, step, part).wait_recv()
                    if step < 3 or (step == 3 and part == way):
                        copy = ring_copy(half, way, step + 1, part)
                        copy.start()
                        started.append(copy)
                    pos = here(half) - step if way == 0 else here(half) + step
                    copy = core_copy(half, slot, pos, part)
                    copy.start()
                    started.append(copy)
                slot += 1
    for copy in started:
        copy.wait_send()
    for half in range(2):
        for index in range(16):
            core_copy(half, index, here(half), 0).wait_recv()

    def project(k, carry):
        weights = wg[k].reshape(256, D)
        part = dot(expanded[k], weights[:, 0:1280])

        @pl.when(k == 0)
        def _():
            acc[...] = part

        @pl.when(k > 0)
        def _():
            acc[...] += part

        return carry

    lax.fori_loop(0, 8, project, 0)
    lane = lax.broadcasted_iota(jnp.int32, (1, QP), 1)
    query = pltpu.roll(acc[:, 0:512].astype(BF16).astype(F32), 32, 1)
    keys = acc[:, 384:896].astype(BF16)
    vals = acc[:, 768:1280].astype(BF16).astype(F32)
    keys = jnp.where((lane >= 32) & (lane < 448), keys.astype(F32), 0.0).astype(BF16)
    mixed = jnp.zeros((PATCHES, QP), F32)
    for h in range(HEADS_HERE):
        in_q = (lane >= 32 + HEAD_DIM * h) & (lane < 32 + HEAD_DIM * (h + 1))
        in_v = (lane >= 64 + HEAD_DIM * h) & (lane < 64 + HEAD_DIM * (h + 1))
        scores = dot(jnp.where(in_q, query, 0.0).astype(BF16), keys, ((1,), (1,))) * HEAD_DIM ** (-0.5)
        top = jnp.max(scores, axis=-1, keepdims=True)
        grown = jnp.exp(scores - top)
        probs = (grown / jnp.sum(grown, axis=-1, keepdims=True)).astype(BF16)
        mixed += dot(probs, jnp.where(in_v, vals, 0.0).astype(BF16))
    heads = pltpu.roll(mixed.astype(BF16).astype(F32), 32, 1)
    heads = jnp.where(lane >= 96, heads, 0.0).astype(BF16)

    def spread_out(k, carry):
        weights = wg[k].reshape(256, D)
        outp[k] = dot(heads, weights[:, 1152:1664], ((1,), (1,))).astype(BF16)
        return carry

    lax.fori_loop(0, 8, spread_out, 0)
    for t in range(13):
        total = None
        for m in range(128 * t // 208, (128 * t + 127) // 208 + 1):
            term = dot(outp[m], strip_pick(128 * t, 128, m, 256), ((1,), (1,)))
            total = term if total is None else total + term
        summed[:, 128 * t : 128 * t + 128] = total.astype(BF16)

    def quarter(q):
        return pl.ds(pl.multiple_of(q * QW, 128), QW)

    def sum_copy(d):
        return remote(
            summed.at[:, quarter((x + d) % NX)], landed.at[d - 1, :, 0:QW], x_send.at[d - 1], x_recv.at[d - 1], xdev(d)
        )

    def tail_copy(d):
        return remote(
            summed.at[:, 4 * QW : D], landed.at[d - 1, :, QW:QP], t_send.at[d - 1], t_recv.at[d - 1], xdev(d)
        )

    for d in (2, 1, 3):
        sum_copy(d).start()

        @pl.when((x + d) % NX == 0)
        def _():
            tail_copy(d).start()

    has_tail = x == 0
    real = (lane < QW) | has_tail
    own = jnp.concatenate([summed[:, quarter(x)], summed[:, 4 * QW : D]], axis=1).astype(F32)
    base = jnp.concatenate([images[:, quarter(x)], images[:, 4 * QW : D]], axis=1).astype(F32)
    gain = jnp.concatenate([mlp_gain[:, quarter(x)], mlp_gain[:, 4 * QW : D]], axis=1)
    gain = jnp.where(real, gain, 0.0)
    for d in (1, 3, 2):
        sum_copy(d).wait()

        @pl.when((x + d) % NX == 0)
        def _():
            tail_copy(d).wait_send()

        @pl.when(has_tail)
        def _():
            tail_copy(d).wait_recv()

    attn = own + landed[0].astype(F32) + landed[1].astype(F32) + landed[2].astype(F32)
    residual = jnp.where(real, base + attn, 0.0)
    residual_out[...] = residual

    def width(q):
        return jnp.where(q == 0, 512.0, 384.0).astype(F32)

    mean_here = jnp.sum(residual, axis=-1, keepdims=True) / width(x)
    off = jnp.where(real, residual - mean_here, 0.0)
    dev_here = jnp.sum(off * off, axis=-1, keepdims=True)
    lane128 = lax.broadcasted_iota(jnp.int32, (1, 128), 1)
    packed = jnp.where(lane128 == 0, mean_here, jnp.where(lane128 == 1, dev_here, 0.0))
    stats[...] = packed.T[0:8, :]

    def stat_copy(d):
        return remote(stats, stats_in.at[d - 1], st_send.at[d - 1], st_recv.at[d - 1], xdev(d))

    for d in (1, 2, 3):
        stat_copy(d).start()
    for d in (1, 2, 3):
        stat_copy(d).wait()
    groups = [(stats[...], width(x))] + [(stats_in[d - 1], width((x + NX - d) % NX)) for d in (1, 2, 3)]
    mean = sum(g[0:1, :] * n for g, n in groups) / float(D)
    var = sum(g[1:2, :] + n * (g[0:1, :] - mean) * (g[0:1, :] - mean) for g, n in groups) / float(D)
    scale = lax.rsqrt(var + 1e-06)
    row = lax.broadcasted_iota(jnp.int32, (128, 256), 0)
    both = jnp.where(row == 0, mean, jnp.where(row == 1, scale, 0.0)).T
    routed_out[...] = ((residual - both[:, 0:1]) * both[:, 1:2] * gain).astype(BF16)


def attention(images, attn_gain, mlp_gain, strips):
    sem = pltpu.SemaphoreType.DMA
    vm = pl.BlockSpec(memory_space=pltpu.VMEM)
    return pl.pallas_call(
        attention_kernel,
        name="attention",
        out_shape=(jax.ShapeDtypeStruct((PATCHES, QP), F32), jax.ShapeDtypeStruct((PATCHES, QP), BF16)),
        in_specs=[vm] * 4,
        out_specs=(vm, vm),
        scratch_shapes=[
            pltpu.VMEM((NZ, NY, 2, ROWS, D), BF16),
            pltpu.VMEM((8, PATCHES, 256), BF16),
            pltpu.VMEM((PATCHES, 1280), F32),
            pltpu.VMEM((8, PATCHES, 256), BF16),
            pltpu.VMEM((PATCHES, D), BF16),
            pltpu.VMEM((3, PATCHES, QP), BF16),
            pltpu.VMEM((8, 256), F32),
            pltpu.VMEM((3, 8, 256), F32),
            sem((2, 7)), sem((2, 7)), sem((2, 2, 8)), sem((2, 2, 8)), sem((2, 16)), sem((2, 16)),
            sem((3,)), sem((3,)), sem((3,)), sem((3,)), sem((3,)), sem((3,)),
        ],
        compiler_params=pltpu.CompilerParams(collective_id=1, has_side_effects=True, vmem_limit_bytes=56 << 20),
    )(images, attn_gain.reshape(1, D), mlp_gain.reshape(1, D), strips)


def make_strips(qkv_weight, proj_weight):
    flat = jnp.concatenate([qkv_weight[0], qkv_weight[1], qkv_weight[2], proj_weight.T], axis=1)
    return jnp.pad(flat, ((0, ROWS - STRIP), (0, 0)))


def gelu_tanh(values):
    return 0.5 * values * (1.0 + jnp.tanh(0.7978845608028654 * (values + 0.044715 * values * values * values)))


def expert_kernel(
    routed, residual, slots, ids, gates, w_in_hbm, w_out_hbm, out,
    w_in, w_out, picked, by_z, by_pair, rows, parts, r1, q, r2a, r2b, sa, sb, r3a, r3b, res, back, by_image, home, final, gathered,
    w_sem, a_send, a_recv, b_send, b_recv, yp_send, yp_recv, xg_send, xg_recv, cg_send, cg_recv,
    r1_send, r1_recv, r2_send, r2_recv, r2y_send, r2y_recv, r3_send, r3_recv, r3y_send, r3y_recv,
    bb_send, bb_recv, aa_send, aa_recv, f_send, f_recv,
):
    x, y, z, c = place()
    par, pair = y % 2, y // 2
    tail = x == 0

    def xdev(d):
        return device((x + d) % NX, y, z, c)

    def ydev(d):
        return device(x, (y + d) % NY, z, c)

    def zdev(d):
        return device(x, y, (z + d) % NZ, c)

    core = device(x, y, z, 1 - c)
    mate = device(x, y + 1 - 2 * par, z, c)

    def quarter(k):
        return pl.ds(pl.multiple_of(k * QW, 128), QW)

    loads = [
        pltpu.make_async_copy(w_in_hbm, w_in, w_sem.at[0]),
        pltpu.make_async_copy(w_out_hbm, w_out, w_sem.at[1]),
    ]
    for load in loads:
        load.start()
    landing = (r2a, sa)
    greet([xdev(d) for d in (1, 2, 3)] + [ydev(d) for d in (2, 4, 6)] + [zdev(d) for d in range(1, NZ)] + [core, mate])

    token = lax.broadcasted_iota(jnp.int32, (PATCHES, 256), 0)
    holds = token == slots[0:1, :]
    picked[...] = dot(jnp.where(holds, 1.0, 0.0).astype(BF16), routed[...], ((0,), (0,))).astype(BF16)

    def a_copy(d):
        to = (z + d) % NZ
        return remote(
            picked.at[pl.ds(pl.multiple_of(to * 32, 32), 32)],
            by_z.at[pl.ds(pl.multiple_of(z * 32, 32), 32)],
            a_send.at[d - 1], a_recv.at[d - 1], zdev(d),
        )

    for d in (4, 3, 5, 2, 6, 1, 7):
        a_copy(d).start()
    own = pl.ds(pl.multiple_of(z * 32, 32), 32)
    by_z[own] = picked[own]

    slot_lane = lax.broadcasted_iota(jnp.int32, (1, 256), 1)
    slot_expert = slot_lane >> 3
    usable = (slot_lane & 7) < slots[1:2, :]
    gate = jnp.where(ids[:, 0:1] == slot_expert, gates[:, 0:1].astype(F32), 0.0)
    gate += jnp.where(ids[:, 1:2] == slot_expert, gates[:, 1:2].astype(F32), 0.0)
    placing = jnp.where(holds & usable, gate, 0.0).astype(BF16)
    r_out = lax.broadcasted_iota(jnp.int32, (256, 256), 0)
    r_in = lax.broadcasted_iota(jnp.int32, (256, 256), 1)
    order = ((r_out >> 6) == ((r_in >> 3) & 3)) & (((r_out >> 3) & 7) == (r_in >> 5)) & ((r_out & 7) == (r_in & 7))
    order = jnp.where(order, 1.0, 0.0).astype(BF16)
    for d in range(1, NZ):
        a_copy(d).wait()
    by_pair[...] = dot(order, by_z[...]).astype(BF16)

    class Both:
        def __init__(self, main, extra, is_tail):
            self.main, self.extra, self.is_tail = main, extra, is_tail

        def start(self):
            self.main.start()
            pl.when(self.is_tail)(self.extra.start)

        def wait_send(self):
            self.main.wait_send()
            pl.when(self.is_tail)(self.extra.wait_send)

        def wait_recv(self):
            self.main.wait_recv()
            pl.when(self.is_tail)(self.extra.wait_recv)

    def pieces(src_main, dst_main, src_extra, dst_extra, send, recv, target, is_tail):
        return Both(
            remote(src_main, dst_main, send.at[0], recv.at[0], target),
            remote(src_extra, dst_extra, send.at[1], recv.at[1], target),
            is_tail,
        )

    def b_copy(i):
        d = 2 * i
        to = ((y + d) % NY) // 2
        src = pl.ds(pl.multiple_of(to * 64, 64), 64)
        dst = pl.ds(pl.multiple_of(pair * 64, 64), 64)
        return pieces(
            by_pair.at[src, 0:QW], rows.at[par, c, dst, quarter(x)],
            by_pair.at[src, QW:QP], rows.at[par, c, dst, 4 * QW : D],
            b_send.at[i - 1], b_recv.at[i - 1], ydev(d), tail,
        )

    for i in (2, 1, 3):
        b_copy(i).start()
    own = pl.ds(pl.multiple_of(pair * 64, 64), 64)
    rows[par, c, own, quarter(x)] = by_pair[own, 0:QW]

    @pl.when(tail)
    def _():
        rows[par, c, own, 4 * QW : D] = by_pair[own, QW:QP]

    for i in (1, 2, 3):
        b_copy(i).wait_recv()

    def same(parity, core_index, q_index, send, recv, target, is_tail):
        main = rows.at[parity, core_index, :, quarter(q_index)]
        extra = rows.at[parity, core_index, :, 4 * QW : D]
        return pieces(main, main, extra, extra, send, recv, target, is_tail)

    mate_copy = same(par, c, x, yp_send, yp_recv, mate, tail)
    mate_copy.start()

    def x_copy(k, d):
        parity = par if k == 0 else 1 - par
        return same(parity, c, x, xg_send.at[k, d - 1], xg_recv.at[k, d - 1], xdev(d), tail)

    def x_arrived(k, d):
        from_tail = (x + NX - d) % NX == 0
        parity = par if k == 0 else 1 - par
        return same(parity, c, x, xg_send.at[k, d - 1], xg_recv.at[k, d - 1], xdev(d), from_tail)

    def core_copy(k, d):
        from_x = (x + NX - d) % NX
        parity = par if k == 0 else 1 - par
        return same(parity, c, from_x, cg_send.at[k, d], cg_recv.at[k, d], core, from_x == 0)

    for d in (2, 1, 3):
        x_copy(0, d).start()
    core_copy(0, 0).start()
    mate_copy.wait_recv()
    for d in (2, 1, 3):
        x_copy(1, d).start()
    core_copy(1, 0).start()
    for d in (1, 3, 2):
        x_arrived(0, d).wait_recv()
        core_copy(0, d).start()
    for load in loads:
        load.wait()

    def expert(parity, core_index):
        hidden = gelu_tanh(dot(rows[parity, core_index], w_in[...])).astype(BF16)
        parts[parity, core_index] = dot(hidden, w_out[...]).astype(BF16)

    def r1_copy(k):
        parity = par if k == 0 else 1 - par
        return remote(parts.at[parity, 1 - c], r1.at[parity], r1_send.at[k], r1_recv.at[k], core)

    for d in range(4):
        core_copy(0, d).wait_recv()
    expert(par, 1 - c)
    r1_copy(0).start()
    expert(par, c)
    for d in (1, 3, 2):
        x_arrived(1, d).wait_recv()
        core_copy(1, d).start()
    for d in range(4):
        core_copy(1, d).wait_recv()
    expert(1 - par, 1 - c)
    r1_copy(1).start()
    expert(1 - par, c)
    r1_copy(0).wait_recv()
    r1_copy(1).wait_recv()

    for parity in range(2):
        q[parity] = (parts[parity, c].astype(F32) + r1[parity].astype(F32)).astype(BF16)

    def r2_copy(d):
        to = (x + d) % NX
        return pieces(
            q.at[:, 0:128, quarter(to)], r2a.at[d - 1, :, :, 0:QW],
            q.at[:, 0:128, 4 * QW : D], r2a.at[d - 1, :, :, QW:QP],
            r2_send.at[d - 1], r2_recv.at[d - 1], xdev(d), to == 0,
        )

    def r2y_copy():
        return remote(q.at[1 - par, 128:256], r2b, r2y_send, r2y_recv, mate)

    def got(copy):
        copy.main.wait_recv()
        pl.when(tail)(copy.extra.wait_recv)

    r2y_copy().start()
    for d in (2, 1, 3):
        r2_copy(d).start()
    r2y_copy().wait_recv()
    sb[...] = (q[par, 128:256].astype(F32) + r2b[...].astype(F32)).astype(BF16)

    def r3_copy(d):
        to = (x + d) % NX
        return pieces(
            sb.at[:, quarter(to)], r3b.at[d - 1, :, 0:QW],
            sb.at[:, 4 * QW : D], r3b.at[d - 1, :, QW:QP],
            r3_send.at[d - 1], r3_recv.at[d - 1], xdev(d), to == 0,
        )

    for d in (2, 1, 3):
        r3_copy(d).start()
    lane = lax.broadcasted_iota(jnp.int32, (1, QP), 1)
    real = (lane < QW) | tail
    for d in (1, 3, 2):
        got(r2_copy(d))
    for parity in range(2):
        total = jnp.concatenate([q[parity, 0:128, quarter(x)], q[parity, 0:128, 4 * QW : D]], axis=1).astype(F32)
        for d in (1, 2, 3):
            total += r2a[d - 1, parity].astype(F32)
        sa[parity] = jnp.where(real, total, 0.0).astype(BF16)

    def r3y_copy():
        return remote(sa.at[1 - par], r3a, r3y_send, r3y_recv, mate)

    r3y_copy().start()
    for d in (1, 3, 2):
        got(r3_copy(d))
    total = jnp.concatenate([sb[:, quarter(x)], sb[:, 4 * QW : D]], axis=1).astype(F32)
    for d in (1, 2, 3):
        total += r3b[d - 1].astype(F32)
    res[128:256] = jnp.where(real, total, 0.0).astype(BF16)
    r3y_copy().wait_recv()
    res[0:128] = (sa[par].astype(F32) + r3a[...].astype(F32)).astype(BF16)

    def bb_copy(i):
        d = 2 * i
        to = ((y + d) % NY) // 2
        return remote(
            res.at[pl.ds(pl.multiple_of(to * 64, 64), 64)], back.at[pl.ds(pl.multiple_of(pair * 64, 64), 64)],
            bb_send.at[i - 1], bb_recv.at[i - 1], ydev(d),
        )

    for i in (2, 1, 3):
        bb_copy(i).start()
    back[own] = res[own]
    for i in (1, 2, 3):
        bb_copy(i).wait_recv()
    by_image[...] = dot(order, back[...], ((0,), (0,))).astype(BF16)

    def aa_copy(d):
        to = (z + d) % NZ
        return remote(
            by_image.at[pl.ds(pl.multiple_of(to * 32, 32), 32)], home.at[pl.ds(pl.multiple_of(z * 32, 32), 32)],
            aa_send.at[d - 1], aa_recv.at[d - 1], zdev(d),
        )

    for d in (4, 3, 5, 2, 6, 1, 7):
        aa_copy(d).start()
    own_z = pl.ds(pl.multiple_of(z * 32, 32), 32)
    home[own_z] = by_image[own_z]
    for d in range(1, NZ):
        aa_copy(d).wait_recv()
    final[...] = (residual[...] + dot(placing, home[...])).astype(BF16)

    def f_copy(d):
        to = pl.ds(pl.multiple_of((x + d) % NX * 64, 64), 64)
        return pieces(
            final.at[to, 0:QW], gathered.at[:, quarter(x)],
            final.at[to, QW:QP], gathered.at[:, 4 * QW : D],
            f_send.at[d - 1], f_recv.at[d - 1], xdev(d), tail,
        )

    for d in (2, 1, 3):
        f_copy(d).start()
    mine = pl.ds(pl.multiple_of(x * 64, 64), 64)
    gathered[:, quarter(x)] = final[mine, 0:QW]

    @pl.when(tail)
    def _():
        gathered[:, 4 * QW : D] = final[mine, QW:QP]

    for d in (1, 3, 2):
        copy = f_copy(d)
        copy.main.wait_recv()
        pl.when((x + NX - d) % NX == 0)(copy.extra.wait_recv)
    out[...] = gathered[...]

    for d in range(1, NZ):
        aa_copy(d).wait_send()
    for i in (1, 2, 3):
        b_copy(i).wait_send()
        bb_copy(i).wait_send()
    mate_copy.wait_send()
    for k in range(2):
        for d in (1, 2, 3):
            x_copy(k, d).wait_send()
        for d in range(4):
            core_copy(k, d).wait_send()
        r1_copy(k).wait_send()
    for d in (1, 2, 3):
        r2_copy(d).wait_send()
        r3_copy(d).wait_send()
        f_copy(d).wait_send()
    r2y_copy().wait_send()
    r3y_copy().wait_send()


def experts(routed, residual, slots, ids, gates, w_in, w_out):
    sem = pltpu.SemaphoreType.DMA
    vm = pl.BlockSpec(memory_space=pltpu.VMEM)
    hbm = pl.BlockSpec(memory_space=pl.ANY)
    v = lambda *s: pltpu.VMEM(s, BF16)
    return pl.pallas_call(
        expert_kernel,
        name="experts",
        out_shape=jax.ShapeDtypeStruct((64, D), BF16),
        in_specs=[vm] * 5 + [hbm] * 2,
        out_specs=vm,
        scratch_shapes=[
            v(D, 512), v(512, D), v(256, QP), v(256, QP), v(256, QP), v(2, 2, 256, D), v(2, 2, 256, D), v(2, 256, D),
            v(2, 256, D), v(3, 2, 128, QP), v(128, D), v(2, 128, QP), v(128, D), v(128, QP), v(3, 128, QP),
            v(256, QP), v(256, QP), v(256, QP), v(256, QP), v(256, QP), v(64, D),
            sem((2,)), sem((7,)), sem((7,)), sem((3, 2)), sem((3, 2)), sem((2,)), sem((2,)),
            sem((2, 3, 2)), sem((2, 3, 2)), sem((2, 4, 2)), sem((2, 4, 2)),
            sem((2,)), sem((2,)), sem((3, 2)), sem((3, 2)), sem, sem, sem((3, 2)), sem((3, 2)), sem, sem,
            sem((3,)), sem((3,)), sem((7,)), sem((7,)), sem((3, 2)), sem((3, 2)),
        ],
        compiler_params=pltpu.CompilerParams(collective_id=2, has_side_effects=True, vmem_limit_bytes=56 << 20),
    )(routed, residual, slots, ids, gates, w_in, w_out)


def on_device(
    images, attn_gain, qkv_weight, proj_weight, mlp_gain, expert_in, expert_out,
    gate_values, expert_ids, kept_patches, kept_counts,
):
    residual, routed = attention(images, attn_gain, mlp_gain, make_strips(qkv_weight, proj_weight))
    slots = jnp.concatenate(
        [kept_patches.reshape(1, 256), jnp.repeat(kept_counts.reshape(1, EXPERTS), 8, axis=1), jnp.zeros((6, 256), jnp.int32)], axis=0
    )
    return experts(routed, residual, slots, expert_ids, gate_values, expert_in, expert_out)


def solution(mesh):
    placed = (
        P("dp", None), P(), P(None, "dp", "mp"), P("mp", "dp"), P(), P(None, ("dp", "mp")), P(("dp", "mp"), None),
        P("dp", None), P("dp", None), P("dp", None, None), P("dp", None),
    )
    return jax.shard_map(on_device, mesh=mesh, in_specs=placed, out_specs=P(("dp", "mp"), None), check_vma=False)
```

```python
import functools

import jax
import jax.numpy as jnp
from jax import lax
from jax.experimental import pallas as pl
from jax.experimental.pallas import tpu as pltpu
from jax.sharding import PartitionSpec as P

MESH = pl.DeviceIdType.MESH
EXPERTS = 32
PATCHES = 256
HEAD_DIM = 104
HEADS_HERE = 4
D = 1664
NX, NY, NZ = 4, 8, 8
STRIP = 13
ROWS = 16
QW = 384
QP = 512
F32 = jnp.float32
BF16 = jnp.bfloat16


def place():
    dp = lax.axis_index("dp")
    return lax.axis_index("mp"), (dp // 2) % NY, dp // (2 * NY), dp % 2


def device(x, y, z, c):
    return ((z * NY + y) * 2 + c, x)


def remote(src, dst, send, recv, target):
    return pltpu.make_async_remote_copy(
        src_ref=src, dst_ref=dst, send_sem=send, recv_sem=recv, device_id=target, device_id_type=MESH
    )


def greet(partners):
    barrier = pltpu.get_barrier_semaphore()
    for partner in partners:
        pl.semaphore_signal(barrier, inc=1, device_id=partner, device_id_type=MESH)
    pl.semaphore_wait(barrier, len(partners))


def gelu_tanh(values):
    return 0.5 * values * (1.0 + jnp.tanh(0.7978845608028654 * (values + 0.044715 * values * values * values)))


def dot(a, b, dims=((1,), (0,))):
    return lax.dot_general(a, b, (dims, ((), ())), preferred_element_type=F32)


CUT = 896
OFFSETS = (0, 1, -1, 2, -2, 3, -3, 4)
CHUNKS = ((0, 1), (1, 3), (3, 5), (5, 8))


def slot_offset(s):
    return jnp.where(s % 2 == 1, (s + 1) // 2, -(s // 2))


def block_kernel(
    images, attn_gain, mlp_gain, qkv, proj, ids_t, gates_t, kept, counts, w_in_hbm, w_out_hbm, out,
    wg0, wg1, scratch_strip, exp0, exp1, acc, outp, summed, landed, stats, stats_in,
    w_in, w_out, picked, by_z, by_pair, rows, parts, r1, q, r2a, r2b, sa, sb, r3a, r3b, res, back, by_image, home, final, gathered,
    s1_send, s1_recv, ring_send, ring_recv, core_send, core_recv, x_send, x_recv, t_send, t_recv, st_send, st_recv,
    w_sem, a_send, a_recv, b_send, b_recv, yp_send, yp_recv, xg_send, xg_recv, cg_send, cg_recv,
    r1_send, r1_recv, r2_send, r2_recv, r2y_send, r2y_recv, r3_send, r3_recv, r3y_send, r3y_recv,
    bb_send, bb_recv, aa_send, aa_recv, f_send, f_recv,
):
    x, y, z, c = place()
    par, pair = y % 2, y // 2
    tail = x == 0

    def xdev(d):
        return device((x + d) % NX, y, z, c)

    def ydev(d):
        return device(x, (y + d) % NY, z, c)

    def zdev(d):
        return device(x, y, (z + d) % NZ, c)

    core = device(x, y, z, 1 - c)
    mate = device(x, y + 1 - 2 * par, z, c)

    def quarter(k):
        return pl.ds(pl.multiple_of(k * QW, 128), QW)

    near = [ydev(1), ydev(NY - 1), zdev(1), zdev(NZ - 1), core, xdev(1), xdev(3), xdev(2)]
    barrier = pltpu.get_barrier_semaphore()
    for partner in near:
        pl.semaphore_signal(barrier, inc=1, device_id=partner, device_id_type=MESH)
    loads = [
        pltpu.make_async_copy(w_in_hbm, w_in, w_sem.at[0]),
        pltpu.make_async_copy(w_out_hbm, w_out, w_sem.at[1]),
    ]
    for load in loads:
        load.start()

    scratch_strip[...] = jnp.zeros_like(scratch_strip)
    for i in range(3):
        scratch_strip[i, 0:STRIP, 0:416] = qkv[i].astype(F32)
    scratch_strip[3, 0:STRIP, 0:416] = proj[...].astype(F32)
    strip = scratch_strip[0]
    for i in range(1, 4):
        strip += pltpu.roll(scratch_strip[i], 416 * i, 1)
    strip = strip.astype(BF16)
    wg0[0, y, c] = strip[:, 0:CUT]
    wg1[z, 0, c] = strip[:, CUT:D]

    pl.semaphore_wait(barrier, len(near))

    def ring(half, stage, sign):
        along_z = (half == 0) == (stage == 1)
        return zdev(sign + NZ) if along_z else ydev(sign + NY)

    def first_copy(half, slot):
        source = 0 if slot < 3 else slot - 2
        if half == 0:
            src, dst = wg0.at[source, y, c], wg0.at[slot, y, c]
        else:
            src, dst = wg1.at[z, source, c], wg1.at[z, slot, c]
        return remote(
            src, dst, s1_send.at[half, slot - 1], s1_recv.at[half, slot - 1], ring(half, 1, -1 if slot % 2 else 1)
        )

    def chunk_ref(half, pos, k):
        low, high = CHUNKS[k]
        if half == 0:
            return wg0.at[low:high, pos % NY, c]
        return wg1.at[pos % NZ, low:high, c]

    def here(half):
        return y if half == 0 else z

    def ring_copy(half, way, step, k):
        pos = here(half) - (step - 1) if way == 0 else here(half) + (step - 1)
        piece = chunk_ref(half, pos + 8, k)
        index = (step - 1) * 4 + k
        return remote(
            piece, piece, ring_send.at[half, way, index], ring_recv.at[half, way, index], ring(half, 2, 1 if way == 0 else -1)
        )

    def core_copy_w(half, slot, pos, k):
        piece = chunk_ref(half, pos + 8, k)
        return remote(piece, piece, core_send.at[half, slot], core_recv.at[half, slot], core)

    started, core_list = [], []

    def go(copy):
        copy.start()
        started.append(copy)

    core_slots = [0, 0]

    def share(half, pos, k):
        copy = core_copy_w(half, core_slots[half], pos, k)
        core_slots[half] += 1
        go(copy)
        core_list.append(copy)

    def begin(k):
        for half in range(2):
            for way in range(2):
                go(ring_copy(half, way, 1, k))
        for half in range(2):
            share(half, here(half), k)

    def last_way(k):
        return 0 if k in (0, 3) else 1

    def advance(k, step):
        for way in range(2):
            if step == 4 and way != last_way(k):
                continue
            for half in range(2):
                ring_copy(half, way, step, k).wait_recv()
                if step < 3 or (step == 3 and way == last_way(k)):
                    go(ring_copy(half, way, step + 1, k))
                share(half, here(half) - step if way == 0 else here(half) + step, k)

    for half in range(2):
        go(first_copy(half, 1))
        go(first_copy(half, 2))
    begin(0)

    values = images[...].astype(F32)
    center = values - jnp.mean(values, axis=-1, keepdims=True)
    spread = jnp.mean(center * center, axis=-1, keepdims=True)
    normed = (center * lax.rsqrt(spread + 1e-06) * attn_gain[...].reshape(1, D)).astype(BF16)

    col = lax.broadcasted_iota(jnp.int32, (1, 256), 1)
    inner = col & (ROWS - 1)
    own_slot = col >> 5
    absolute = jnp.where(inner < STRIP, STRIP * (col >> 4) + inner, -4096)
    turned = ((y + NY + slot_offset(own_slot)) % NY) * 2 + ((col >> 4) & 1)
    relative = jnp.where(inner < STRIP, STRIP * turned + inner, -4096)

    def strip_pick(first, count, target):
        feature = lax.broadcasted_iota(jnp.int32, (count, 256), 0) + first
        return jnp.where(feature == target, 1.0, 0.0).astype(BF16)

    def expand(m):
        low = (208 * m) // 128 * 128
        wide = min(384, D - low)
        exp0[m] = dot(normed[:, low : low + wide], strip_pick(low - 208 * m, wide, absolute)).astype(BF16)
        exp1[m] = dot(normed[:, low : low + wide], strip_pick(low - 208 * m, wide, relative)).astype(BF16)

    for half in range(2):
        for slot in (1, 2):
            first_copy(half, slot).wait_recv()
            go(first_copy(half, slot + 2))
    begin(1)
    advance(0, 1)
    for half in range(2):
        for slot in (3, 4):
            first_copy(half, slot).wait_recv()
            go(first_copy(half, slot + 2))
    begin(2)
    advance(1, 1)
    advance(0, 2)
    expand(0)
    for half in range(2):
        for slot in (5, 6):
            first_copy(half, slot).wait_recv()
        go(first_copy(half, 7))
    advance(2, 1)
    advance(1, 2)
    expand(1)
    for half in range(2):
        first_copy(half, 7).wait_recv()
    begin(3)
    advance(0, 3)
    expand(2)
    for wave in range(4, 8):
        for k in (3, 2, 1, 0):
            step = wave - k
            if 1 <= step <= 4:
                advance(k, step)
        if wave < 7:
            expand(2 * wave - 5)
            if 2 * wave - 4 < 8:
                expand(2 * wave - 4)

    slot_col = lax.broadcasted_iota(jnp.int32, (256, 32), 0)
    expert_col = lax.broadcasted_iota(jnp.int32, (256, 32), 1)
    of_expert = jnp.where((slot_col >> 3) == expert_col, 1.0, 0.0)
    patch8 = dot(of_expert.astype(BF16), kept[...].astype(F32).astype(BF16), ((1,), (1,)))
    which = (lax.broadcasted_iota(jnp.int32, (256, 8), 0) & 7) == lax.broadcasted_iota(jnp.int32, (256, 8), 1)
    patch = jnp.sum(jnp.where(which, patch8, 0.0), axis=1, keepdims=True)
    valid = jnp.sum(of_expert * counts[...].astype(F32), axis=1, keepdims=True)
    lane128 = lax.broadcasted_iota(jnp.int32, (1, 128), 1)
    slot_rows = jnp.where(lane128 == 0, patch, jnp.where(lane128 == 1, valid, 0.0)).T
    row128 = lax.broadcasted_iota(jnp.int32, (128, 256), 0)
    meta = jnp.where(row128 == 0, ids_t[0:1, :].astype(F32), 0.0)
    meta = jnp.where(row128 == 1, ids_t[1:2, :].astype(F32), meta)
    meta = jnp.where(row128 == 2, gates_t[0:1, :].astype(F32), meta)
    meta = jnp.where(row128 == 3, gates_t[1:2, :].astype(F32), meta).T
    token = lax.broadcasted_iota(jnp.int32, (PATCHES, 256), 0)
    holds = token == slot_rows[0:1, :].astype(jnp.int32)
    slot_lane = lax.broadcasted_iota(jnp.int32, (1, 256), 1)
    slot_expert = (slot_lane >> 3).astype(F32)
    usable = (slot_lane & 7).astype(F32) < slot_rows[1:2, :]
    gate = jnp.where(meta[:, 0:1] == slot_expert, meta[:, 2:3], 0.0)
    gate += jnp.where(meta[:, 1:2] == slot_expert, meta[:, 3:4], 0.0)
    placing = jnp.where(holds & usable, gate, 0.0).astype(BF16)
    choosing = jnp.where(holds, 1.0, 0.0).astype(BF16)
    r_out = lax.broadcasted_iota(jnp.int32, (256, 256), 0)
    r_in = lax.broadcasted_iota(jnp.int32, (256, 256), 1)
    order = ((r_out >> 6) == ((r_in >> 3) & 3)) & (((r_out >> 3) & 7) == (r_in >> 5)) & ((r_out & 7) == (r_in & 7))
    order = jnp.where(order, 1.0, 0.0).astype(BF16)

    for copy in core_list:
        copy.wait_recv()

    acc[...] = jnp.zeros_like(acc)

    def project(k, carry):
        acc[:, 0:CUT] += dot(exp0[(z + NZ + slot_offset(k)) % NZ], wg0[k].reshape(256, CUT))
        acc[:, CUT:1280] += dot(exp1[k], wg1[k].reshape(256, D - CUT)[:, 0 : 1280 - CUT])
        return carry

    lax.fori_loop(0, 8, project, 0)
    lane = lax.broadcasted_iota(jnp.int32, (1, QP), 1)
    keys = acc[:, 384:896].astype(BF16).astype(F32)
    keys = jnp.where((lane >= 32) & (lane < 448), keys, 0.0).astype(BF16)
    vals = acc[:, 768:1280].astype(BF16).astype(F32)

    def sum_copy(h, d):
        return remote(
            summed.at[128 * h : 128 * h + 128, quarter((x + d) % NX)], landed.at[h, d - 1, :, 0:QW],
            x_send.at[h, d - 1], x_recv.at[h, d - 1], xdev(d),
        )

    def tail_copy(h, d):
        return remote(
            summed.at[128 * h : 128 * h + 128, 4 * QW : D], landed.at[h, d - 1, :, QW:QP],
            t_send.at[h, d - 1], t_recv.at[h, d - 1], xdev(d),
        )

    for half_rows in range(2):
        low = 128 * half_rows
        query = pltpu.roll(acc[low : low + 128, 0:512].astype(BF16).astype(F32), 32, 1)
        mixed = jnp.zeros((128, QP), F32)
        for h in range(HEADS_HERE):
            in_q = (lane >= 32 + HEAD_DIM * h) & (lane < 32 + HEAD_DIM * (h + 1))
            in_v = (lane >= 64 + HEAD_DIM * h) & (lane < 64 + HEAD_DIM * (h + 1))
            scores = dot(jnp.where(in_q, query, 0.0).astype(BF16), keys, ((1,), (1,))) * HEAD_DIM ** (-0.5)
            top = jnp.max(scores, axis=-1, keepdims=True)
            grown = jnp.exp(scores - top)
            probs = (grown / jnp.sum(grown, axis=-1, keepdims=True)).astype(BF16)
            mixed += dot(probs, jnp.where(in_v, vals, 0.0).astype(BF16))
        heads = pltpu.roll(mixed.astype(BF16).astype(F32), 32, 1)
        heads = jnp.where(lane >= 96, heads, 0.0).astype(BF16)

        def spread_out(k, carry, low=low, heads=heads):
            weights = wg1[k].reshape(256, D - CUT)[:, 1152 - CUT : D - CUT]
            outp[k, low : low + 128, :] = dot(heads, weights, ((1,), (1,))).astype(BF16)
            return carry

        lax.fori_loop(0, 8, spread_out, 0)
        for t in range(13):
            total = None
            for m in range(128 * t // 208, (128 * t + 127) // 208 + 1):
                term = dot(outp[m, low : low + 128, :], strip_pick(128 * t - 208 * m, 128, relative), ((1,), (1,)))
                total = term if total is None else total + term
            summed[low : low + 128, 128 * t : 128 * t + 128] = total.astype(BF16)
        for d in (2, 1, 3):
            go(sum_copy(half_rows, d))
            pl.when((x + d) % NX == 0)(tail_copy(half_rows, d).start)

    real = (lane < QW) | tail
    own = jnp.concatenate([summed[:, quarter(x)], summed[:, 4 * QW : D]], axis=1).astype(F32)
    base = jnp.concatenate([images[:, quarter(x)], images[:, 4 * QW : D]], axis=1).astype(F32)
    gain = jnp.concatenate([mlp_gain[quarter(x)], mlp_gain[4 * QW : D]]).reshape(1, QP)
    gain = jnp.where(real, gain, 0.0)
    for h in range(2):
        for d in (1, 3, 2):
            sum_copy(h, d).wait_recv()
            pl.when(tail)(tail_copy(h, d).wait_recv)

    attn = own
    for d in (1, 2, 3):
        attn += jnp.concatenate([landed[0, d - 1], landed[1, d - 1]], axis=0).astype(F32)
    residual = jnp.where(real, base + attn, 0.0)

    def width(k):
        return jnp.where(k == 0, 512.0, 384.0).astype(F32)

    mean_here = jnp.sum(residual, axis=-1, keepdims=True) / width(x)
    off = jnp.where(real, residual - mean_here, 0.0)
    dev_here = jnp.sum(off * off, axis=-1, keepdims=True)
    stats[...] = jnp.where(lane128 == 0, mean_here, jnp.where(lane128 == 1, dev_here, 0.0)).T[0:8, :]

    def stat_copy(d):
        return remote(stats, stats_in.at[d - 1], st_send.at[d - 1], st_recv.at[d - 1], xdev(d))

    for d in (2, 1, 3):
        go(stat_copy(d))
    for d in (1, 3, 2):
        stat_copy(d).wait_recv()
    groups = [(stats[...], width(x))] + [(stats_in[d - 1], width((x + NX - d) % NX)) for d in (1, 2, 3)]
    mean = sum(g[0:1, :] * n for g, n in groups) / float(D)
    var = sum(g[1:2, :] + n * (g[0:1, :] - mean) * (g[0:1, :] - mean) for g, n in groups) / float(D)
    scale = lax.rsqrt(var + 1e-06)
    both = jnp.where(row128 == 0, mean, jnp.where(row128 == 1, scale, 0.0)).T
    routed = ((residual - both[:, 0:1]) * both[:, 1:2] * gain).astype(BF16)
    picked[...] = dot(choosing, routed, ((0,), (0,))).astype(BF16)

    def a_copy(d):
        to = (z + d) % NZ
        return remote(
            picked.at[pl.ds(pl.multiple_of(to * 32, 32), 32)],
            by_z.at[pl.ds(pl.multiple_of(z * 32, 32), 32)],
            a_send.at[d - 1], a_recv.at[d - 1], zdev(d),
        )

    for d in (4, 3, 5, 2, 6, 1, 7):
        a_copy(d).start()
    own = pl.ds(pl.multiple_of(z * 32, 32), 32)
    by_z[own] = picked[own]

    for d in range(1, NZ):
        a_copy(d).wait()
    by_pair[...] = dot(order, by_z[...]).astype(BF16)

    class Both:
        def __init__(self, main, extra, is_tail):
            self.main, self.extra, self.is_tail = main, extra, is_tail

        def start(self):
            self.main.start()
            pl.when(self.is_tail)(self.extra.start)

        def wait_send(self):
            self.main.wait_send()
            pl.when(self.is_tail)(self.extra.wait_send)

        def wait_recv(self):
            self.main.wait_recv()
            pl.when(self.is_tail)(self.extra.wait_recv)

    def pieces(src_main, dst_main, src_extra, dst_extra, send, recv, target, is_tail):
        return Both(
            remote(src_main, dst_main, send.at[0], recv.at[0], target),
            remote(src_extra, dst_extra, send.at[1], recv.at[1], target),
            is_tail,
        )

    def b_copy(i):
        d = 2 * i
        to = ((y + d) % NY) // 2
        src = pl.ds(pl.multiple_of(to * 64, 64), 64)
        dst = pl.ds(pl.multiple_of(pair * 64, 64), 64)
        return pieces(
            by_pair.at[src, 0:QW], rows.at[par, c, dst, quarter(x)],
            by_pair.at[src, QW:QP], rows.at[par, c, dst, 4 * QW : D],
            b_send.at[i - 1], b_recv.at[i - 1], ydev(d), tail,
        )

    for i in (2, 1, 3):
        b_copy(i).start()
    own = pl.ds(pl.multiple_of(pair * 64, 64), 64)
    rows[par, c, own, quarter(x)] = by_pair[own, 0:QW]

    @pl.when(tail)
    def _():
        rows[par, c, own, 4 * QW : D] = by_pair[own, QW:QP]

    for i in (1, 2, 3):
        b_copy(i).wait_recv()

    def same(parity, core_index, q_index, send, recv, target, is_tail):
        main = rows.at[parity, core_index, :, quarter(q_index)]
        extra = rows.at[parity, core_index, :, 4 * QW : D]
        return pieces(main, main, extra, extra, send, recv, target, is_tail)

    mate_copy = same(par, c, x, yp_send, yp_recv, mate, tail)
    mate_copy.start()

    def x_copy(k, d):
        parity = par if k == 0 else 1 - par
        return same(parity, c, x, xg_send.at[k, d - 1], xg_recv.at[k, d - 1], xdev(d), tail)

    def x_arrived(k, d):
        from_tail = (x + NX - d) % NX == 0
        parity = par if k == 0 else 1 - par
        return same(parity, c, x, xg_send.at[k, d - 1], xg_recv.at[k, d - 1], xdev(d), from_tail)

    def core_copy(k, d):
        from_x = (x + NX - d) % NX
        parity = par if k == 0 else 1 - par
        return same(parity, c, from_x, cg_send.at[k, d], cg_recv.at[k, d], core, from_x == 0)

    for d in (2, 1, 3):
        x_copy(0, d).start()
    core_copy(0, 0).start()
    mate_copy.wait_recv()
    for d in (2, 1, 3):
        x_copy(1, d).start()
    core_copy(1, 0).start()
    for d in (1, 3, 2):
        x_arrived(0, d).wait_recv()
        core_copy(0, d).start()
    for load in loads:
        load.wait()

    def expert(parity, core_index):
        hidden = gelu_tanh(dot(rows[parity, core_index], w_in[...])).astype(BF16)
        parts[parity, core_index] = dot(hidden, w_out[...]).astype(BF16)

    def r1_copy(k):
        parity = par if k == 0 else 1 - par
        return remote(parts.at[parity, 1 - c], r1.at[parity], r1_send.at[k], r1_recv.at[k], core)

    for d in range(4):
        core_copy(0, d).wait_recv()
    expert(par, 1 - c)
    r1_copy(0).start()
    expert(par, c)
    for d in (1, 3, 2):
        x_arrived(1, d).wait_recv()
        core_copy(1, d).start()
    for d in range(4):
        core_copy(1, d).wait_recv()
    expert(1 - par, 1 - c)
    r1_copy(1).start()
    expert(1 - par, c)
    r1_copy(0).wait_recv()
    r1_copy(1).wait_recv()

    for parity in range(2):
        q[parity] = (parts[parity, c].astype(F32) + r1[parity].astype(F32)).astype(BF16)

    def r2_copy(d):
        to = (x + d) % NX
        return pieces(
            q.at[:, 0:128, quarter(to)], r2a.at[d - 1, :, :, 0:QW],
            q.at[:, 0:128, 4 * QW : D], r2a.at[d - 1, :, :, QW:QP],
            r2_send.at[d - 1], r2_recv.at[d - 1], xdev(d), to == 0,
        )

    def r2y_copy():
        return remote(q.at[1 - par, 128:256], r2b, r2y_send, r2y_recv, mate)

    def got(copy):
        copy.main.wait_recv()
        pl.when(tail)(copy.extra.wait_recv)

    r2y_copy().start()
    for d in (2, 1, 3):
        r2_copy(d).start()
    r2y_copy().wait_recv()
    sb[...] = (q[par, 128:256].astype(F32) + r2b[...].astype(F32)).astype(BF16)

    def r3_copy(d):
        to = (x + d) % NX
        return pieces(
            sb.at[:, quarter(to)], r3b.at[d - 1, :, 0:QW],
            sb.at[:, 4 * QW : D], r3b.at[d - 1, :, QW:QP],
            r3_send.at[d - 1], r3_recv.at[d - 1], xdev(d), to == 0,
        )

    for d in (2, 1, 3):
        r3_copy(d).start()
    for d in (1, 3, 2):
        got(r2_copy(d))
    for parity in range(2):
        total = jnp.concatenate([q[parity, 0:128, quarter(x)], q[parity, 0:128, 4 * QW : D]], axis=1).astype(F32)
        for d in (1, 2, 3):
            total += r2a[d - 1, parity].astype(F32)
        sa[parity] = jnp.where(real, total, 0.0).astype(BF16)

    def r3y_copy():
        return remote(sa.at[1 - par], r3a, r3y_send, r3y_recv, mate)

    r3y_copy().start()
    for d in (1, 3, 2):
        got(r3_copy(d))
    total = jnp.concatenate([sb[:, quarter(x)], sb[:, 4 * QW : D]], axis=1).astype(F32)
    for d in (1, 2, 3):
        total += r3b[d - 1].astype(F32)
    res[128:256] = jnp.where(real, total, 0.0).astype(BF16)
    r3y_copy().wait_recv()
    res[0:128] = (sa[par].astype(F32) + r3a[...].astype(F32)).astype(BF16)

    def bb_copy(i):
        d = 2 * i
        to = ((y + d) % NY) // 2
        return remote(
            res.at[pl.ds(pl.multiple_of(to * 64, 64), 64)], back.at[pl.ds(pl.multiple_of(pair * 64, 64), 64)],
            bb_send.at[i - 1], bb_recv.at[i - 1], ydev(d),
        )

    for i in (2, 1, 3):
        bb_copy(i).start()
    back[own] = res[own]
    for i in (1, 2, 3):
        bb_copy(i).wait_recv()
    by_image[...] = dot(order, back[...], ((0,), (0,))).astype(BF16)

    def aa_copy(d):
        to = (z + d) % NZ
        return remote(
            by_image.at[pl.ds(pl.multiple_of(to * 32, 32), 32)], home.at[pl.ds(pl.multiple_of(z * 32, 32), 32)],
            aa_send.at[d - 1], aa_recv.at[d - 1], zdev(d),
        )

    for d in (4, 3, 5, 2, 6, 1, 7):
        aa_copy(d).start()
    own_z = pl.ds(pl.multiple_of(z * 32, 32), 32)
    home[own_z] = by_image[own_z]
    for d in range(1, NZ):
        aa_copy(d).wait_recv()
    final[...] = (residual + dot(placing, home[...])).astype(BF16)

    def f_copy(d):
        to = pl.ds(pl.multiple_of((x + d) % NX * 64, 64), 64)
        return pieces(
            final.at[to, 0:QW], gathered.at[:, quarter(x)],
            final.at[to, QW:QP], gathered.at[:, 4 * QW : D],
            f_send.at[d - 1], f_recv.at[d - 1], xdev(d), tail,
        )

    for d in (2, 1, 3):
        f_copy(d).start()
    mine = pl.ds(pl.multiple_of(x * 64, 64), 64)
    gathered[:, quarter(x)] = final[mine, 0:QW]

    @pl.when(tail)
    def _():
        gathered[:, 4 * QW : D] = final[mine, QW:QP]

    for d in (1, 3, 2):
        copy = f_copy(d)
        copy.main.wait_recv()
        pl.when((x + NX - d) % NX == 0)(copy.extra.wait_recv)
    out[...] = gathered[...]

    for copy in started:
        copy.wait_send()
    for h in range(2):
        for d in (1, 2, 3):
            pl.when((x + d) % NX == 0)(tail_copy(h, d).wait_send)
    for d in range(1, NZ):
        aa_copy(d).wait_send()
    for i in (1, 2, 3):
        b_copy(i).wait_send()
        bb_copy(i).wait_send()
    mate_copy.wait_send()
    for k in range(2):
        for d in (1, 2, 3):
            x_copy(k, d).wait_send()
        for d in range(4):
            core_copy(k, d).wait_send()
        r1_copy(k).wait_send()
    for d in (1, 2, 3):
        r2_copy(d).wait_send()
        r3_copy(d).wait_send()
        f_copy(d).wait_send()
    r2y_copy().wait_send()
    r3y_copy().wait_send()


def block(images, attn_gain, mlp_gain, qkv, proj_t, ids_t, gates_t, kept, counts, w_in, w_out):
    sem = pltpu.SemaphoreType.DMA
    vm = pl.BlockSpec(memory_space=pltpu.VMEM)
    hbm = pl.BlockSpec(memory_space=pl.ANY)

    def v(*shape, kind=BF16):
        return pltpu.VMEM(shape, kind)

    return pl.pallas_call(
        block_kernel,
        name="block",
        out_shape=jax.ShapeDtypeStruct((64, D), BF16),
        in_specs=[vm] * 9 + [hbm] * 2,
        out_specs=vm,
        scratch_shapes=[
            v(8, NY, 2, ROWS, CUT), v(NZ, 8, 2, ROWS, D - CUT), v(4, ROWS, D, kind=F32),
            v(8, PATCHES, 256), v(8, PATCHES, 256), v(PATCHES, 1280, kind=F32), v(8, PATCHES, 256), v(PATCHES, D),
            v(2, 3, 128, QP), v(8, 256, kind=F32), v(3, 8, 256, kind=F32),
            v(D, 512), v(512, D), v(256, QP), v(256, QP), v(256, QP), v(2, 2, 256, D), v(2, 2, 256, D), v(2, 256, D),
            v(2, 256, D), v(3, 2, 128, QP), v(128, D), v(2, 128, QP), v(128, D), v(128, QP), v(3, 128, QP),
            v(256, QP), v(256, QP), v(256, QP), v(256, QP), v(256, QP), v(64, D),
            sem((2, 7)), sem((2, 7)), sem((2, 2, 16)), sem((2, 2, 16)), sem((2, 32)), sem((2, 32)),
            sem((2, 3)), sem((2, 3)), sem((2, 3)), sem((2, 3)), sem((3,)), sem((3,)),
            sem((2,)), sem((7,)), sem((7,)), sem((3, 2)), sem((3, 2)), sem((2,)), sem((2,)),
            sem((2, 3, 2)), sem((2, 3, 2)), sem((2, 4, 2)), sem((2, 4, 2)),
            sem((2,)), sem((2,)), sem((3, 2)), sem((3, 2)), sem, sem, sem((3, 2)), sem((3, 2)), sem, sem,
            sem((3,)), sem((3,)), sem((7,)), sem((7,)), sem((3, 2)), sem((3, 2)),
        ],
        compiler_params=pltpu.CompilerParams(collective_id=1, has_side_effects=True, vmem_limit_bytes=56 << 20),
    )(images, attn_gain, mlp_gain, qkv, proj_t, ids_t, gates_t, kept, counts, w_in, w_out)


def on_device(
    images, attn_gain, qkv_weight, proj_weight, mlp_gain, expert_in, expert_out,
    gate_values, expert_ids, kept_patches, kept_counts,
):
    return block(
        images, attn_gain, mlp_gain, qkv_weight, proj_weight.T, expert_ids.T, gate_values.T,
        kept_patches[0].T, kept_counts, expert_in, expert_out,
    )


def solution(mesh):
    placed = (
        P("dp", None), P(), P(None, "dp", "mp"), P("mp", "dp"), P(), P(None, ("dp", "mp")), P(("dp", "mp"), None),
        P("dp", None), P("dp", None), P("dp", None, None), P("dp", None),
    )
    return jax.shard_map(on_device, mesh=mesh, in_specs=placed, out_specs=P(("dp", "mp"), None), check_vma=False)
```

```python
import functools

import jax
import jax.numpy as jnp
from jax import lax
from jax.experimental import pallas as pl
from jax.experimental.pallas import tpu as pltpu
from jax.sharding import PartitionSpec as P

MESH = pl.DeviceIdType.MESH
EXPERTS = 32
PATCHES = 256
HEAD_DIM = 104
HEADS_HERE = 4
D = 1664
NX, NY, NZ = 4, 8, 8
STRIP = 13
ROWS = 16
QW = 384
QP = 512
F32 = jnp.float32
BF16 = jnp.bfloat16


def place():
    dp = lax.axis_index("dp")
    return lax.axis_index("mp"), (dp // 2) % NY, dp // (2 * NY), dp % 2


def device(x, y, z, c):
    return ((z * NY + y) * 2 + c, x)


def remote(src, dst, send, recv, target):
    return pltpu.make_async_remote_copy(
        src_ref=src, dst_ref=dst, send_sem=send, recv_sem=recv, device_id=target, device_id_type=MESH
    )


def greet(partners):
    barrier = pltpu.get_barrier_semaphore()
    for partner in partners:
        pl.semaphore_signal(barrier, inc=1, device_id=partner, device_id_type=MESH)
    pl.semaphore_wait(barrier, len(partners))


def gelu_tanh(values):
    return 0.5 * values * (1.0 + jnp.tanh(0.7978845608028654 * (values + 0.044715 * values * values * values)))


def dot(a, b, dims=((1,), (0,))):
    return lax.dot_general(a, b, (dims, ((), ())), preferred_element_type=F32)


FAR = sorted(((i, d) for i in range(4) for d in range(8) if (i, d) != (0, 0)), key=lambda s: -(min(2 * s[0], 8 - 2 * s[0]) + min(s[1], 8 - s[1])))
FIRST = 176
CUT = 896
OFFSETS = (0, 1, -1, 2, -2, 3, -3, 4)
CHUNKS = ((0, 1), (1, 3), (3, 5), (5, 7), (7, 8))
ROUTE = (
    ("start", 0), ("first", 1), ("first", 2), ("start", 1), (1, 1, 0), (0, 1, 0), ("first", 3), ("first", 4), ("start", 2),
    (1, 1, 1), (0, 1, 1), (1, 2, 0), (0, 2, 0), ("first", 5), ("first", 6), ("start", 3), (1, 1, 2), (0, 1, 2), (1, 2, 1),
    (0, 2, 1), (1, 3, 0), (0, 3, 0), ("first", 7), ("start", 4), (0, 1, 3), (1, 1, 3), (0, 2, 2), (1, 2, 2), (0, 3, 1),
    (1, 3, 1), (0, 1, 4), (1, 4, 0), (1, 1, 4), (0, 2, 3), (1, 2, 3), (0, 3, 2), (0, 2, 4), (1, 3, 2), (0, 3, 3), (1, 4, 1),
    (1, 2, 4), (0, 3, 4), (1, 3, 3), (1, 4, 2), (0, 4, 3), (1, 3, 4), (0, 4, 4),
)


def slot_offset(s):
    return jnp.where(s % 2 == 1, (s + 1) // 2, -(s // 2))


def block_kernel(
    images_hbm, attn_gain_hbm, mlp_gain_hbm, qkv_hbm, proj_hbm, ids_hbm, gates_hbm, kept_hbm, counts_hbm,
    w_in_hbm, w_out_hbm, out,
    images, attn_gain, mlp_gain, qkv, proj, ids_t, gates_t, kept, counts,
    wg0, wg1, scratch_strip, exp0, exp1, acc, outp, summed, landed, stats, stats_in,
    w_in, w_out, picked, arrived, rows, parts, r1, q, r2a, r2c, r2b, sa, sb, r3a, r3b, returning, home, final, gathered,
    s1_send, s1_recv, ring_send, ring_recv, core_send, core_recv, x_send, x_recv, t_send, t_recv, st_send, st_recv,
    w_sem, a_send, a_recv, yp_send, yp_recv, xg_send, xg_recv, cg_send, cg_recv,
    r1_send, r1_recv, r2_send, r2_recv, r2c_send, r2c_recv, r2y_send, r2y_recv, r3_send, r3_recv, r3y_send, r3y_recv,
    aa_send, aa_recv, f_send, f_recv,
):
    x, y, z, c = place()
    par, pair = y % 2, y // 2
    tail = x == 0

    def xdev(d):
        return device((x + d) % NX, y, z, c)

    def ydev(d):
        return device(x, (y + d) % NY, z, c)

    def zdev(d):
        return device(x, y, (z + d) % NZ, c)

    core = device(x, y, z, 1 - c)
    mate = device(x, y + 1 - 2 * par, z, c)

    def quarter(k):
        return pl.ds(pl.multiple_of(k * QW, 128), QW)

    near = [ydev(1), ydev(NY - 1), zdev(1), zdev(NZ - 1), core, xdev(1), xdev(3), xdev(2)]
    barrier = pltpu.get_barrier_semaphore()
    for partner in near:
        pl.semaphore_signal(barrier, inc=1, device_id=partner, device_id_type=MESH)
    arguments = (
        (qkv_hbm, qkv), (proj_hbm, proj), (kept_hbm, kept), (counts_hbm, counts), (ids_hbm, ids_t), (gates_hbm, gates_t),
        (images_hbm, images), (attn_gain_hbm, attn_gain), (mlp_gain_hbm, mlp_gain), (w_in_hbm, w_in), (w_out_hbm, w_out),
    )
    loads = [pltpu.make_async_copy(src, dst, w_sem.at[i]) for i, (src, dst) in enumerate(arguments)]
    for load in loads:
        load.start()
    for load in loads[0:6]:
        load.wait()

    scratch_strip[...] = jnp.zeros_like(scratch_strip)
    for i in range(3):
        scratch_strip[i, 0:STRIP, 0:416] = qkv[i].astype(F32)
    scratch_strip[3, 0:STRIP, 0:416] = proj[...].astype(F32)
    strip = scratch_strip[0]
    for i in range(1, 4):
        strip += pltpu.roll(scratch_strip[i], 416 * i, 1)
    strip = strip.astype(BF16)
    wg0[0, y, c] = strip[:, 0:CUT]
    wg1[z, 0, c] = strip[:, CUT:D]

    slot_col = lax.broadcasted_iota(jnp.int32, (256, 32), 0)
    expert_col = lax.broadcasted_iota(jnp.int32, (256, 32), 1)
    of_expert = jnp.where((slot_col >> 3) == expert_col, 1.0, 0.0)
    patch8 = dot(of_expert.astype(BF16), kept[...].astype(F32).astype(BF16), ((1,), (1,)))
    which = (lax.broadcasted_iota(jnp.int32, (256, 8), 0) & 7) == lax.broadcasted_iota(jnp.int32, (256, 8), 1)
    patch = jnp.sum(jnp.where(which, patch8, 0.0), axis=1, keepdims=True)
    valid = jnp.sum(of_expert * counts[...].astype(F32), axis=1, keepdims=True)
    lane128 = lax.broadcasted_iota(jnp.int32, (1, 128), 1)
    slot_rows = jnp.where(lane128 == 0, patch, jnp.where(lane128 == 1, valid, 0.0)).T
    row128 = lax.broadcasted_iota(jnp.int32, (128, 256), 0)
    meta = jnp.where(row128 == 0, ids_t[0:1, :].astype(F32), 0.0)
    meta = jnp.where(row128 == 1, ids_t[1:2, :].astype(F32), meta)
    meta = jnp.where(row128 == 2, gates_t[0:1, :].astype(F32), meta)
    meta = jnp.where(row128 == 3, gates_t[1:2, :].astype(F32), meta).T
    token = lax.broadcasted_iota(jnp.int32, (PATCHES, 256), 0)
    holds = token == slot_rows[0:1, :].astype(jnp.int32)
    slot_lane = lax.broadcasted_iota(jnp.int32, (1, 256), 1)
    slot_expert = (slot_lane >> 3).astype(F32)
    usable = (slot_lane & 7).astype(F32) < slot_rows[1:2, :]
    gate = jnp.where(meta[:, 0:1] == slot_expert, meta[:, 2:3], 0.0)
    gate += jnp.where(meta[:, 1:2] == slot_expert, meta[:, 3:4], 0.0)
    placing = jnp.where(holds & usable, gate, 0.0).astype(BF16)
    choosing = jnp.where(holds, 1.0, 0.0).astype(BF16)

    acc[...] = jnp.zeros_like(acc)
    pl.semaphore_wait(barrier, len(near))

    def ring(half, stage, sign):
        along_z = (half == 0) == (stage == 1)
        return zdev(sign + NZ) if along_z else ydev(sign + NY)

    def first_copy(half, slot):
        source = 0 if slot < 3 else slot - 2
        if half == 0:
            src, dst = wg0.at[source, y, c], wg0.at[slot, y, c]
        else:
            src, dst = wg1.at[z, source, c], wg1.at[z, slot, c]
        return remote(
            src, dst, s1_send.at[half, slot - 1], s1_recv.at[half, slot - 1], ring(half, 1, -1 if slot % 2 else 1)
        )

    def chunk_ref(half, pos, k):
        low, high = CHUNKS[k]
        if half == 0:
            return wg0.at[low:high, pos % NY, c]
        return wg1.at[pos % NZ, low:high, c]

    def here(half):
        return y if half == 0 else z

    def ring_copy(half, way, step, k):
        pos = here(half) - (step - 1) if way == 0 else here(half) + (step - 1)
        piece = chunk_ref(half, pos + 8, k)
        index = (step - 1) * 5 + k
        return remote(
            piece, piece, ring_send.at[half, way, index], ring_recv.at[half, way, index], ring(half, 2, 1 if way == 0 else -1)
        )

    def core_copy_w(half, slot, pos, k):
        piece = chunk_ref(half, pos + 8, k)
        return remote(piece, piece, core_send.at[half, slot], core_recv.at[half, slot], core)

    started, core_list = [], [[] for _ in CHUNKS]

    def go(copy):
        copy.start()
        started.append(copy)

    core_slots = [0, 0]

    def share(half, pos, k):
        copy = core_copy_w(half, core_slots[half], pos, k)
        core_slots[half] += 1
        go(copy)
        core_list[k].append(copy)

    def begin(k):
        for half in range(2):
            for way in range(2):
                go(ring_copy(half, way, 1, k))
        for half in range(2):
            share(half, here(half), k)

    def last_way(k):
        return 1 if k < 3 else 0

    def advance(way, step, k):
        for half in range(2):
            ring_copy(half, way, step, k).wait_recv()
            if step < 3 or (step == 3 and way == last_way(k)):
                go(ring_copy(half, way, step + 1, k))
            share(half, here(half) - step if way == 0 else here(half) + step, k)

    col = lax.broadcasted_iota(jnp.int32, (1, 256), 1)
    inner = col & (ROWS - 1)
    own_slot = col >> 5
    absolute = jnp.where(inner < STRIP, STRIP * (col >> 4) + inner, -4096)
    turned = ((y + NY + slot_offset(own_slot)) % NY) * 2 + ((col >> 4) & 1)
    relative = jnp.where(inner < STRIP, STRIP * turned + inner, -4096)

    def strip_pick(first, count, target):
        feature = lax.broadcasted_iota(jnp.int32, (count, 256), 0) + first
        return jnp.where(feature == target, 1.0, 0.0).astype(BF16)

    def expand(m):
        low = (208 * m) // 128 * 128
        wide = min(384, D - low)
        exp0[m] = dot(normed[:, low : low + wide], strip_pick(low - 208 * m, wide, absolute)).astype(BF16)
        exp1[m] = dot(normed[:, low : low + wide], strip_pick(low - 208 * m, wide, relative)).astype(BF16)

    def project(k):
        acc[:, 0:CUT] += dot(exp0[(z + NZ + OFFSETS[k]) % NZ], wg0[k].reshape(256, CUT))

    def finish(k):
        for copy in core_list[k]:
            copy.wait_recv()
        for slot in range(*CHUNKS[k]):
            project(slot)

    for half in range(2):
        go(first_copy(half, 1))
        go(first_copy(half, 2))
    for at, entry in enumerate(ROUTE):
        if entry[0] == "start":
            begin(entry[1])
        elif entry[0] == "first":
            for half in range(2):
                first_copy(half, entry[1]).wait_recv()
                if entry[1] <= 5:
                    go(first_copy(half, entry[1] + 2))
        else:
            advance(*entry)
        if at == 0:
            for load in loads[6:9]:
                load.wait()
            values = images[...].astype(F32)
            center = values - jnp.mean(values, axis=-1, keepdims=True)
            spread = jnp.mean(center * center, axis=-1, keepdims=True)
            normed = (center * lax.rsqrt(spread + 1e-06) * attn_gain[...].reshape(1, D)).astype(BF16)
        if 8 <= at < 24 and at % 2 == 0:
            expand((at - 8) // 2)
        if at in (38, 42, 45):
            finish((38, 42, 45).index(at))
    finish(3)
    finish(4)
    for k in range(8):
        part = dot(exp1[k], wg1[k].reshape(256, D - CUT)[:, 0 : 1280 - CUT])
        late = part if k == 0 else late + part
    acc[:, CUT:1280] = late
    lane = lax.broadcasted_iota(jnp.int32, (1, QP), 1)
    keys = acc[:, 384:896].astype(BF16).astype(F32)
    keys = jnp.where((lane >= 32) & (lane < 448), keys, 0.0).astype(BF16)
    vals = acc[:, 768:1280].astype(BF16).astype(F32)

    def sum_copy(h, d):
        return remote(
            summed.at[128 * h : 128 * h + 128, quarter((x + d) % NX)], landed.at[h, d - 1, :, 0:QW],
            x_send.at[h, d - 1], x_recv.at[h, d - 1], xdev(d),
        )

    def tail_copy(h, d):
        return remote(
            summed.at[128 * h : 128 * h + 128, 4 * QW : D], landed.at[h, d - 1, :, QW:QP],
            t_send.at[h, d - 1], t_recv.at[h, d - 1], xdev(d),
        )

    for half_rows in range(2):
        low = 128 * half_rows
        query = pltpu.roll(acc[low : low + 128, 0:512].astype(BF16).astype(F32), 32, 1)
        mixed = jnp.zeros((128, QP), F32)
        for h in range(HEADS_HERE):
            in_q = (lane >= 32 + HEAD_DIM * h) & (lane < 32 + HEAD_DIM * (h + 1))
            in_v = (lane >= 64 + HEAD_DIM * h) & (lane < 64 + HEAD_DIM * (h + 1))
            scores = dot(jnp.where(in_q, query, 0.0).astype(BF16), keys, ((1,), (1,))) * HEAD_DIM ** (-0.5)
            top = jnp.max(scores, axis=-1, keepdims=True)
            grown = jnp.exp(scores - top)
            probs = (grown / jnp.sum(grown, axis=-1, keepdims=True)).astype(BF16)
            mixed += dot(probs, jnp.where(in_v, vals, 0.0).astype(BF16))
        heads = pltpu.roll(mixed.astype(BF16).astype(F32), 32, 1)
        heads = jnp.where(lane >= 96, heads, 0.0).astype(BF16)

        def spread_out(k, carry, low=low, heads=heads):
            weights = wg1[k].reshape(256, D - CUT)[:, 1152 - CUT : D - CUT]
            outp[k, low : low + 128, :] = dot(heads, weights, ((1,), (1,))).astype(BF16)
            return carry

        lax.fori_loop(0, 8, spread_out, 0)
        for t in range(13):
            total = None
            for m in range(128 * t // 208, (128 * t + 127) // 208 + 1):
                term = dot(outp[m, low : low + 128, :], strip_pick(128 * t - 208 * m, 128, relative), ((1,), (1,)))
                total = term if total is None else total + term
            summed[low : low + 128, 128 * t : 128 * t + 128] = total.astype(BF16)
        for d in (2, 1, 3):
            go(sum_copy(half_rows, d))
            pl.when((x + d) % NX == 0)(tail_copy(half_rows, d).start)

    real = (lane < QW) | tail
    own = jnp.concatenate([summed[:, quarter(x)], summed[:, 4 * QW : D]], axis=1).astype(F32)
    base = jnp.concatenate([images[:, quarter(x)], images[:, 4 * QW : D]], axis=1).astype(F32)
    gain = jnp.concatenate([mlp_gain[quarter(x)], mlp_gain[4 * QW : D]]).reshape(1, QP)
    gain = jnp.where(real, gain, 0.0)
    for h in range(2):
        for d in (1, 3, 2):
            sum_copy(h, d).wait_recv()
            pl.when(tail)(tail_copy(h, d).wait_recv)

    attn = own
    for d in (1, 2, 3):
        attn += jnp.concatenate([landed[0, d - 1], landed[1, d - 1]], axis=0).astype(F32)
    residual = jnp.where(real, base + attn, 0.0)

    def width(k):
        return jnp.where(k == 0, 512.0, 384.0).astype(F32)

    mean_here = jnp.sum(residual, axis=-1, keepdims=True) / width(x)
    off = jnp.where(real, residual - mean_here, 0.0)
    dev_here = jnp.sum(off * off, axis=-1, keepdims=True)
    stats[...] = jnp.where(lane128 == 0, mean_here, jnp.where(lane128 == 1, dev_here, 0.0)).T[0:8, :]

    def stat_copy(d):
        return remote(stats, stats_in.at[d - 1], st_send.at[d - 1], st_recv.at[d - 1], xdev(d))

    for d in (2, 1, 3):
        go(stat_copy(d))
    for d in (1, 3, 2):
        stat_copy(d).wait_recv()
    groups = [(stats[...], width(x))] + [(stats_in[d - 1], width((x + NX - d) % NX)) for d in (1, 2, 3)]
    mean = sum(g[0:1, :] * n for g, n in groups) / float(D)
    var = sum(g[1:2, :] + n * (g[0:1, :] - mean) * (g[0:1, :] - mean) for g, n in groups) / float(D)
    scale = lax.rsqrt(var + 1e-06)
    both = jnp.where(row128 == 0, mean, jnp.where(row128 == 1, scale, 0.0)).T
    routed = ((residual - both[:, 0:1]) * both[:, 1:2] * gain).astype(BF16)
    chosen = dot(choosing, routed, ((0,), (0,)))

    def folded(value):
        return jnp.concatenate([value[:, 0:256].reshape(32, 8, 256), value[:, 256:512].reshape(32, 8, 256)], axis=1).astype(BF16)

    def unfolded(value):
        value = value.reshape(32, 16, 256).astype(F32)
        return value[:, 0:8].reshape(256, 256).astype(BF16), value[:, 8:16].reshape(256, 256).astype(BF16)

    picked[...] = folded(chosen)

    def a_copy(i, d):
        to_y, to_z = (y + 2 * i) % NY, (z + d) % NZ
        return remote(
            picked.at[4 * to_z + to_y // 2], arrived.at[pair, z], a_send.at[i, d], a_recv.at[i, d], device(x, to_y, to_z, c)
        )

    for i, d in FAR:
        a_copy(i, d).start()
    arrived[pair, z] = picked[4 * z + pair]

    class Both:
        def __init__(self, main, extra, is_tail):
            self.main, self.extra, self.is_tail = main, extra, is_tail

        def start(self):
            self.main.start()
            pl.when(self.is_tail)(self.extra.start)

        def wait_send(self):
            self.main.wait_send()
            pl.when(self.is_tail)(self.extra.wait_send)

        def wait_recv(self):
            self.main.wait_recv()
            pl.when(self.is_tail)(self.extra.wait_recv)

    def pieces(src_main, dst_main, src_extra, dst_extra, send, recv, target, is_tail):
        return Both(
            remote(src_main, dst_main, send.at[0], recv.at[0], target),
            remote(src_extra, dst_extra, send.at[1], recv.at[1], target),
            is_tail,
        )

    for i, d in FAR[::-1]:
        a_copy(i, d).wait_recv()
    left, right = unfolded(arrived[...])
    rows[par, c, :, quarter(x)] = jnp.concatenate([left, right[:, 0:128]], axis=1)

    @pl.when(tail)
    def _():
        rows[par, c, :, 4 * QW : D] = right[:, 128:256]

    def same(parity, core_index, q_index, send, recv, target, is_tail):
        main = rows.at[parity, core_index, :, quarter(q_index)]
        extra = rows.at[parity, core_index, :, 4 * QW : D]
        return pieces(main, main, extra, extra, send, recv, target, is_tail)

    mate_copy = same(par, c, x, yp_send, yp_recv, mate, tail)
    mate_copy.start()

    def x_copy(k, d):
        parity = par if k == 0 else 1 - par
        return same(parity, c, x, xg_send.at[k, d - 1], xg_recv.at[k, d - 1], xdev(d), tail)

    def x_arrived(k, d):
        from_tail = (x + NX - d) % NX == 0
        parity = par if k == 0 else 1 - par
        return same(parity, c, x, xg_send.at[k, d - 1], xg_recv.at[k, d - 1], xdev(d), from_tail)

    def core_copy(k, d):
        from_x = (x + NX - d) % NX
        parity = par if k == 0 else 1 - par
        return same(parity, c, from_x, cg_send.at[k, d], cg_recv.at[k, d], core, from_x == 0)

    for d in (2, 1, 3):
        x_copy(0, d).start()
    core_copy(0, 0).start()
    mate_copy.wait_recv()
    for d in (2, 1, 3):
        x_copy(1, d).start()
    core_copy(1, 0).start()
    for d in (1, 3, 2):
        x_arrived(0, d).wait_recv()
        core_copy(0, d).start()
    for load in loads[9:]:
        load.wait()

    def expert(parity, core_index):
        hidden = gelu_tanh(dot(rows[parity, core_index], w_in[...])).astype(BF16)
        parts[parity, core_index] = dot(hidden, w_out[...]).astype(BF16)

    def r1_copy(k):
        parity = par if k == 0 else 1 - par
        return remote(parts.at[parity, 1 - c], r1.at[parity], r1_send.at[k], r1_recv.at[k], core)

    for d in range(4):
        core_copy(0, d).wait_recv()
    expert(par, 1 - c)
    r1_copy(0).start()
    expert(par, c)
    for d in (1, 3, 2):
        x_arrived(1, d).wait_recv()
        core_copy(1, d).start()

    def both_cores(parity):
        q[parity] = (parts[parity, c].astype(F32) + r1[parity].astype(F32)).astype(BF16)

    def quarters(src, rows_of, dst, send, recv, d):
        to = (x + d) % NX
        return pieces(
            src.at[rows_of, quarter(to)], dst.at[d - 1, :, 0:QW], src.at[rows_of, 4 * QW : D], dst.at[d - 1, :, QW:QP],
            send.at[d - 1], recv.at[d - 1], xdev(d), to == 0,
        )

    def got(copy):
        copy.main.wait_recv()
        pl.when(tail)(copy.extra.wait_recv)

    def own_sum_copy(d):
        return quarters(q.at[par], pl.ds(0, FIRST), r2a, r2_send, r2_recv, d)

    def mate_sum_copy(d):
        return quarters(q.at[1 - par], pl.ds(0, FIRST), r2c, r2c_send, r2c_recv, d)

    def rest_copy():
        return remote(q.at[1 - par, FIRST:256], r2b, r2y_send, r2y_recv, mate)

    def late_copy(d):
        return quarters(sb, pl.ds(0, 256 - FIRST), r3b, r3_send, r3_recv, d)

    def summed_copy():
        return remote(sa, r3a, r3y_send, r3y_recv, mate)

    def mine_of(value):
        return jnp.concatenate([value[:, quarter(x)], value[:, 4 * QW : D]], axis=1).astype(F32)

    r1_copy(0).wait_recv()
    both_cores(par)
    for d in (2, 1, 3):
        own_sum_copy(d).start()
    for d in range(4):
        core_copy(1, d).wait_recv()
    expert(1 - par, 1 - c)
    r1_copy(1).start()
    expert(1 - par, c)
    r1_copy(1).wait_recv()
    both_cores(1 - par)
    rest_copy().start()
    for d in (2, 1, 3):
        mate_sum_copy(d).start()
    for d in (1, 3, 2):
        got(own_sum_copy(d))
    own_total = mine_of(q.at[par, 0:FIRST])
    for d in (1, 2, 3):
        own_total += r2a[d - 1].astype(F32)
    rest_copy().wait_recv()
    sb[...] = (q[par, FIRST:256].astype(F32) + r2b[...].astype(F32)).astype(BF16)
    for d in (2, 1, 3):
        late_copy(d).start()
    for d in (1, 3, 2):
        got(mate_sum_copy(d))
    total = mine_of(q.at[1 - par, 0:FIRST])
    for d in (1, 2, 3):
        total += r2c[d - 1].astype(F32)
    sa[...] = jnp.where(real, total, 0.0).astype(BF16)
    summed_copy().start()
    total = mine_of(sb)
    for d in (1, 3, 2):
        got(late_copy(d))
        total += r3b[d - 1].astype(F32)
    low_rows = jnp.where(real, total, 0.0)
    summed_copy().wait_recv()
    result = jnp.concatenate([jnp.where(real, own_total + r3a[...].astype(F32), 0.0), low_rows], axis=0)

    returning[...] = folded(result).reshape(4, 8, 16, 256)

    def aa_copy(i, d):
        to_y, to_z = (y + 2 * i) % NY, (z + d) % NZ
        return remote(
            returning.at[to_y // 2, to_z], home.at[4 * z + pair], aa_send.at[i, d], aa_recv.at[i, d], device(x, to_y, to_z, c)
        )

    for i, d in FAR:
        aa_copy(i, d).start()
    home[4 * z + pair] = returning[pair, z]
    for i, d in FAR[::-1]:
        aa_copy(i, d).wait_recv()
    left, right = unfolded(home[...])
    final[...] = (residual + jnp.concatenate([dot(placing, left), dot(placing, right)], axis=1)).astype(BF16)

    def f_copy(d):
        to = pl.ds(pl.multiple_of((x + d) % NX * 64, 64), 64)
        return pieces(
            final.at[to, 0:QW], gathered.at[:, quarter(x)],
            final.at[to, QW:QP], gathered.at[:, 4 * QW : D],
            f_send.at[d - 1], f_recv.at[d - 1], xdev(d), tail,
        )

    for d in (2, 1, 3):
        f_copy(d).start()
    mine = pl.ds(pl.multiple_of(x * 64, 64), 64)
    gathered[:, quarter(x)] = final[mine, 0:QW]

    @pl.when(tail)
    def _():
        gathered[:, 4 * QW : D] = final[mine, QW:QP]

    for d in (1, 3, 2):
        copy = f_copy(d)
        copy.main.wait_recv()
        pl.when((x + NX - d) % NX == 0)(copy.extra.wait_recv)
    out[...] = gathered[...]

    for copy in started:
        copy.wait_send()
    for h in range(2):
        for d in (1, 2, 3):
            pl.when((x + d) % NX == 0)(tail_copy(h, d).wait_send)
    for i, d in FAR:
        a_copy(i, d).wait_send()
        aa_copy(i, d).wait_send()
    mate_copy.wait_send()
    for k in range(2):
        for d in (1, 2, 3):
            x_copy(k, d).wait_send()
        for d in range(4):
            core_copy(k, d).wait_send()
        r1_copy(k).wait_send()
    for d in (1, 2, 3):
        own_sum_copy(d).wait_send()
        mate_sum_copy(d).wait_send()
        late_copy(d).wait_send()
        f_copy(d).wait_send()
    rest_copy().wait_send()
    summed_copy().wait_send()


def block(images, attn_gain, mlp_gain, qkv, proj_t, ids_t, gates_t, kept, counts, w_in, w_out):
    sem = pltpu.SemaphoreType.DMA
    vm = pl.BlockSpec(memory_space=pltpu.VMEM)
    hbm = pl.BlockSpec(memory_space=pl.ANY)

    def v(*shape, kind=BF16):
        return pltpu.VMEM(shape, kind)

    return pl.pallas_call(
        block_kernel,
        name="block",
        out_shape=jax.ShapeDtypeStruct((64, D), BF16),
        in_specs=[hbm] * 11,
        out_specs=vm,
        scratch_shapes=[
            v(PATCHES, D), v(D, kind=F32), v(D, kind=F32), v(3, STRIP, 416), v(STRIP, 416),
            v(2, PATCHES, kind=jnp.int32), v(2, PATCHES), v(8, EXPERTS, kind=jnp.int32), v(1, EXPERTS, kind=jnp.int32),
            v(8, NY, 2, ROWS, CUT), v(NZ, 8, 2, ROWS, D - CUT), v(4, ROWS, D, kind=F32),
            v(8, PATCHES, 256), v(8, PATCHES, 256), v(PATCHES, 1280, kind=F32), v(8, PATCHES, 256), v(PATCHES, D),
            v(2, 3, 128, QP), v(8, 256, kind=F32), v(3, 8, 256, kind=F32),
            v(D, 512), v(512, D), v(32, 16, 256), v(4, 8, 16, 256), v(2, 2, 256, D), v(2, 2, 256, D), v(2, 256, D),
            v(2, 256, D), v(3, FIRST, QP), v(3, FIRST, QP), v(256 - FIRST, D), v(FIRST, QP), v(256 - FIRST, D), v(FIRST, QP), v(3, 256 - FIRST, QP),
            v(4, 8, 16, 256), v(32, 16, 256), v(256, QP), v(64, D),
            sem((2, 7)), sem((2, 7)), sem((2, 2, 20)), sem((2, 2, 20)), sem((2, 40)), sem((2, 40)),
            sem((2, 3)), sem((2, 3)), sem((2, 3)), sem((2, 3)), sem((3,)), sem((3,)),
            sem((11,)), sem((4, 8)), sem((4, 8)), sem((2,)), sem((2,)),
            sem((2, 3, 2)), sem((2, 3, 2)), sem((2, 4, 2)), sem((2, 4, 2)),
            sem((2,)), sem((2,)), sem((3, 2)), sem((3, 2)), sem((3, 2)), sem((3, 2)), sem, sem, sem((3, 2)), sem((3, 2)), sem, sem,
            sem((4, 8)), sem((4, 8)), sem((3, 2)), sem((3, 2)),
        ],
        compiler_params=pltpu.CompilerParams(collective_id=1, has_side_effects=True, vmem_limit_bytes=56 << 20),
    )(images, attn_gain, mlp_gain, qkv, proj_t, ids_t, gates_t, kept, counts, w_in, w_out)


def on_device(
    images, attn_gain, qkv_weight, proj_weight, mlp_gain, expert_in, expert_out,
    gate_values, expert_ids, kept_patches, kept_counts,
):
    return block(
        images, attn_gain, mlp_gain, qkv_weight, proj_weight.T, expert_ids.T, gate_values.T,
        kept_patches[0].T, kept_counts, expert_in, expert_out,
    )


def solution(mesh):
    placed = (
        P("dp", None), P(), P(None, "dp", "mp"), P("mp", "dp"), P(), P(None, ("dp", "mp")), P(("dp", "mp"), None),
        P("dp", None), P("dp", None), P("dp", None, None), P("dp", None),
    )
    return jax.shard_map(on_device, mesh=mesh, in_specs=placed, out_specs=P(("dp", "mp"), None), check_vma=False)
```

```python
import functools

import jax
import jax.numpy as jnp
from jax import lax
from jax.experimental import pallas as pl
from jax.experimental.pallas import tpu as pltpu
from jax.sharding import PartitionSpec as P

MESH = pl.DeviceIdType.MESH
EXPERTS = 32
PATCHES = 256
HEAD_DIM = 104
HEADS_HERE = 4
D = 1664
NX, NY, NZ = 4, 8, 8
STRIP = 13
ROWS = 16
QW = 384
QP = 512
F32 = jnp.float32
BF16 = jnp.bfloat16


def place():
    dp = lax.axis_index("dp")
    return lax.axis_index("mp"), (dp // 2) % NY, dp // (2 * NY), dp % 2


def device(x, y, z, c):
    return ((z * NY + y) * 2 + c, x)


def remote(src, dst, send, recv, target):
    return pltpu.make_async_remote_copy(
        src_ref=src, dst_ref=dst, send_sem=send, recv_sem=recv, device_id=target, device_id_type=MESH
    )


def greet(partners):
    barrier = pltpu.get_barrier_semaphore()
    for partner in partners:
        pl.semaphore_signal(barrier, inc=1, device_id=partner, device_id_type=MESH)
    pl.semaphore_wait(barrier, len(partners))


def gelu_tanh(values):
    return 0.5 * values * (1.0 + jnp.tanh(0.7978845608028654 * (values + 0.044715 * values * values * values)))


def dot(a, b, dims=((1,), (0,))):
    return lax.dot_general(a, b, (dims, ((), ())), preferred_element_type=F32)


FAR = sorted(((i, d) for i in range(4) for d in range(8) if (i, d) != (0, 0)), key=lambda s: -(min(2 * s[0], 8 - 2 * s[0]) + min(s[1], 8 - s[1])))
FIRST = 160
HALF = FIRST // 2
CUT = 896
OFFSETS = (0, 1, -1, 2, -2, 3, -3, 4)
CHUNKS = ((0, 1), (1, 3), (3, 5), (5, 7), (7, 8))
ROUTE = (
    ("start", 0), ("first", 1), ("first", 2), ("start", 1), (1, 1, 0), (0, 1, 0), ("first", 3), ("first", 4), ("start", 2),
    (1, 1, 1), (0, 1, 1), (1, 2, 0), (0, 2, 0), ("first", 5), ("first", 6), ("start", 3), (1, 1, 2), (0, 1, 2), (1, 2, 1),
    (0, 2, 1), (1, 3, 0), (0, 3, 0), ("first", 7), ("start", 4), (0, 1, 3), (1, 1, 3), (0, 2, 2), (1, 2, 2), (0, 3, 1),
    (1, 3, 1), (0, 1, 4), (1, 4, 0), (1, 1, 4), (0, 2, 3), (1, 2, 3), (0, 3, 2), (0, 2, 4), (1, 3, 2), (0, 3, 3), (1, 4, 1),
    (1, 2, 4), (0, 3, 4), (1, 3, 3), (1, 4, 2), (0, 4, 3), (1, 3, 4), (0, 4, 4),
)


def slot_offset(s):
    return jnp.where(s % 2 == 1, (s + 1) // 2, -(s // 2))


def block_kernel(
    images_hbm, attn_gain_hbm, mlp_gain_hbm, qkv_hbm, proj_hbm, ids_hbm, gates_hbm, kept_hbm, counts_hbm,
    w_in_hbm, w_out_hbm, out,
    images, attn_gain, mlp_gain, qkv, proj, ids_t, gates_t, kept, counts,
    wg0, wg1, scratch_strip, exp0, exp1, acc, outp, summed, landed,
    w_in, w_out, picked, arrived, rows, parts, r1, q, r2a, r2c, r2b, sa, sb, r3a, r3b, returning, home, final, gathered,
    s1_send, s1_recv, ring_send, ring_recv, core_send, core_recv, x_send, x_recv, t_send, t_recv,
    w_sem, a_send, a_recv, yp_send, yp_recv, xg_send, xg_recv, cg_send, cg_recv,
    r1_send, r1_recv, r2_send, r2_recv, r2c_send, r2c_recv, r2y_send, r2y_recv, r3_send, r3_recv, r3y_send, r3y_recv,
    aa_send, aa_recv, f_send, f_recv,
):
    x, y, z, c = place()
    par, pair = y % 2, y // 2
    tail = x == 0

    def xdev(d):
        return device((x + d) % NX, y, z, c)

    def ydev(d):
        return device(x, (y + d) % NY, z, c)

    def zdev(d):
        return device(x, y, (z + d) % NZ, c)

    core = device(x, y, z, 1 - c)
    mate = device(x, y + 1 - 2 * par, z, c)

    def quarter(k):
        return pl.ds(pl.multiple_of(k * QW, 128), QW)

    near = [ydev(1), ydev(NY - 1), zdev(1), zdev(NZ - 1), core, xdev(1), xdev(3), xdev(2)]
    barrier = pltpu.get_barrier_semaphore()
    for partner in near:
        pl.semaphore_signal(barrier, inc=1, device_id=partner, device_id_type=MESH)
    arguments = (
        (qkv_hbm, qkv), (proj_hbm, proj), (kept_hbm, kept), (counts_hbm, counts), (ids_hbm, ids_t), (gates_hbm, gates_t),
        (images_hbm, images), (attn_gain_hbm, attn_gain), (mlp_gain_hbm, mlp_gain), (w_in_hbm, w_in), (w_out_hbm, w_out),
    )
    loads = [pltpu.make_async_copy(src, dst, w_sem.at[i]) for i, (src, dst) in enumerate(arguments)]
    for load in loads:
        load.start()
    for load in loads[0:6]:
        load.wait()

    scratch_strip[...] = jnp.zeros_like(scratch_strip)
    for i in range(3):
        scratch_strip[i, 0:STRIP, 0:416] = qkv[i].astype(F32)
    scratch_strip[3, 0:STRIP, 0:416] = proj[...].astype(F32)
    strip = scratch_strip[0]
    for i in range(1, 4):
        strip += pltpu.roll(scratch_strip[i], 416 * i, 1)
    strip = strip.astype(BF16)
    wg0[0, y, c] = strip[:, 0:CUT]
    wg1[z, 0, c] = strip[:, CUT:D]

    slot_col = lax.broadcasted_iota(jnp.int32, (256, 32), 0)
    expert_col = lax.broadcasted_iota(jnp.int32, (256, 32), 1)
    of_expert = jnp.where((slot_col >> 3) == expert_col, 1.0, 0.0)
    patch8 = dot(of_expert.astype(BF16), kept[...].astype(F32).astype(BF16), ((1,), (1,)))
    which = (lax.broadcasted_iota(jnp.int32, (256, 8), 0) & 7) == lax.broadcasted_iota(jnp.int32, (256, 8), 1)
    patch = jnp.sum(jnp.where(which, patch8, 0.0), axis=1, keepdims=True)
    valid = jnp.sum(of_expert * counts[...].astype(F32), axis=1, keepdims=True)
    lane128 = lax.broadcasted_iota(jnp.int32, (1, 128), 1)
    slot_rows = jnp.where(lane128 == 0, patch, jnp.where(lane128 == 1, valid, 0.0)).T
    row128 = lax.broadcasted_iota(jnp.int32, (128, 256), 0)
    meta = jnp.where(row128 == 0, ids_t[0:1, :].astype(F32), 0.0)
    meta = jnp.where(row128 == 1, ids_t[1:2, :].astype(F32), meta)
    meta = jnp.where(row128 == 2, gates_t[0:1, :].astype(F32), meta)
    meta = jnp.where(row128 == 3, gates_t[1:2, :].astype(F32), meta).T
    token = lax.broadcasted_iota(jnp.int32, (PATCHES, 256), 0)
    holds = token == slot_rows[0:1, :].astype(jnp.int32)
    slot_lane = lax.broadcasted_iota(jnp.int32, (1, 256), 1)
    slot_expert = (slot_lane >> 3).astype(F32)
    usable = (slot_lane & 7).astype(F32) < slot_rows[1:2, :]
    gate = jnp.where(meta[:, 0:1] == slot_expert, meta[:, 2:3], 0.0)
    gate += jnp.where(meta[:, 1:2] == slot_expert, meta[:, 3:4], 0.0)
    placing = jnp.where(holds & usable, gate, 0.0).astype(BF16)
    choosing = jnp.where(holds, 1.0, 0.0).astype(BF16)

    acc[...] = jnp.zeros_like(acc)
    pl.semaphore_wait(barrier, len(near))

    def ring(half, stage, sign):
        along_z = (half == 0) == (stage == 1)
        return zdev(sign + NZ) if along_z else ydev(sign + NY)

    def first_copy(half, slot):
        source = 0 if slot < 3 else slot - 2
        if half == 0:
            src, dst = wg0.at[source, y, c], wg0.at[slot, y, c]
        else:
            src, dst = wg1.at[z, source, c], wg1.at[z, slot, c]
        return remote(
            src, dst, s1_send.at[half, slot - 1], s1_recv.at[half, slot - 1], ring(half, 1, -1 if slot % 2 else 1)
        )

    def chunk_ref(half, pos, k):
        low, high = CHUNKS[k]
        if half == 0:
            return wg0.at[low:high, pos % NY, c]
        return wg1.at[pos % NZ, low:high, c]

    def here(half):
        return y if half == 0 else z

    def ring_copy(half, way, step, k):
        pos = here(half) - (step - 1) if way == 0 else here(half) + (step - 1)
        piece = chunk_ref(half, pos + 8, k)
        index = (step - 1) * 5 + k
        return remote(
            piece, piece, ring_send.at[half, way, index], ring_recv.at[half, way, index], ring(half, 2, 1 if way == 0 else -1)
        )

    def core_copy_w(half, slot, pos, k):
        piece = chunk_ref(half, pos + 8, k)
        return remote(piece, piece, core_send.at[half, slot], core_recv.at[half, slot], core)

    started, core_list = [], [[] for _ in CHUNKS]

    def go(copy):
        copy.start()
        started.append(copy)

    core_slots = [0, 0]

    def share(half, pos, k):
        copy = core_copy_w(half, core_slots[half], pos, k)
        core_slots[half] += 1
        go(copy)
        core_list[k].append(copy)

    def begin(k):
        for half in range(2):
            for way in range(2):
                go(ring_copy(half, way, 1, k))
        for half in range(2):
            share(half, here(half), k)

    def last_way(k):
        return 1 if k < 3 else 0

    def advance(way, step, k):
        for half in range(2):
            ring_copy(half, way, step, k).wait_recv()
            if step < 3 or (step == 3 and way == last_way(k)):
                go(ring_copy(half, way, step + 1, k))
            share(half, here(half) - step if way == 0 else here(half) + step, k)

    col = lax.broadcasted_iota(jnp.int32, (1, 256), 1)
    inner = col & (ROWS - 1)
    own_slot = col >> 5
    absolute = jnp.where(inner < STRIP, STRIP * (col >> 4) + inner, -4096)
    turned = ((y + NY + slot_offset(own_slot)) % NY) * 2 + ((col >> 4) & 1)
    relative = jnp.where(inner < STRIP, STRIP * turned + inner, -4096)

    def strip_pick(first, count, target):
        feature = lax.broadcasted_iota(jnp.int32, (count, 256), 0) + first
        return jnp.where(feature == target, 1.0, 0.0).astype(BF16)

    def expand(m):
        low = (208 * m) // 128 * 128
        wide = min(384, D - low)
        exp0[m] = dot(normed[:, low : low + wide], strip_pick(low - 208 * m, wide, absolute)).astype(BF16)
        exp1[m] = dot(normed[:, low : low + wide], strip_pick(low - 208 * m, wide, relative)).astype(BF16)

    def project(k):
        acc[:, 0:CUT] += dot(exp0[(z + NZ + OFFSETS[k]) % NZ], wg0[k].reshape(256, CUT))

    def finish(k):
        for copy in core_list[k]:
            copy.wait_recv()
        for slot in range(*CHUNKS[k]):
            project(slot)

    for half in range(2):
        go(first_copy(half, 1))
        go(first_copy(half, 2))
    for at, entry in enumerate(ROUTE):
        if entry[0] == "start":
            begin(entry[1])
        elif entry[0] == "first":
            for half in range(2):
                first_copy(half, entry[1]).wait_recv()
                if entry[1] <= 5:
                    go(first_copy(half, entry[1] + 2))
        else:
            advance(*entry)
        if at == 0:
            for load in loads[6:9]:
                load.wait()
            values = images[...].astype(F32)
            image_mean = jnp.mean(values, axis=-1, keepdims=True)
            center = values - image_mean
            spread = jnp.mean(center * center, axis=-1, keepdims=True)
            normed = (center * lax.rsqrt(spread + 1e-06) * attn_gain[...].reshape(1, D)).astype(BF16)
        if 8 <= at < 24 and at % 2 == 0:
            expand((at - 8) // 2)
        if at in (38, 42, 45):
            finish((38, 42, 45).index(at))
    finish(3)
    finish(4)
    for k in range(8):
        part = dot(exp1[k], wg1[k].reshape(256, D - CUT)[:, 0 : 1280 - CUT])
        late = part if k == 0 else late + part
    acc[:, CUT:1280] = late
    lane = lax.broadcasted_iota(jnp.int32, (1, QP), 1)
    keys = acc[:, 384:896].astype(BF16).astype(F32)
    keys = jnp.where((lane >= 32) & (lane < 448), keys, 0.0).T.astype(BF16)
    vals = acc[:, 768:1280].astype(BF16).astype(F32)

    def sum_copy(h, d):
        return remote(
            summed.at[128 * h : 128 * h + 128, quarter((x + d) % NX)], landed.at[h, d - 1, :, 0:QW],
            x_send.at[h, d - 1], x_recv.at[h, d - 1], xdev(d),
        )

    def tail_copy(h, d):
        return remote(
            summed.at[128 * h : 128 * h + 128, 4 * QW : D], landed.at[h, d - 1, :, QW:QP],
            t_send.at[h, d - 1], t_recv.at[h, d - 1], xdev(d),
        )

    for half_rows in range(2):
        low = 128 * half_rows
        query = pltpu.roll(acc[low : low + 128, 0:512].astype(BF16).astype(F32), 32, 1)
        mixed = jnp.zeros((128, QP), F32)
        for h in range(HEADS_HERE):
            in_q = (lane >= 32 + HEAD_DIM * h) & (lane < 32 + HEAD_DIM * (h + 1))
            in_v = (lane >= 64 + HEAD_DIM * h) & (lane < 64 + HEAD_DIM * (h + 1))
            scores = dot(jnp.where(in_q, query, 0.0).astype(BF16), keys) * HEAD_DIM ** (-0.5)
            top = jnp.max(scores, axis=-1, keepdims=True)
            grown = jnp.exp(scores - top)
            probs = (grown / jnp.sum(grown, axis=-1, keepdims=True)).astype(BF16)
            mixed += dot(probs, jnp.where(in_v, vals, 0.0).astype(BF16))
        heads = pltpu.roll(mixed.astype(BF16).astype(F32), 32, 1)
        heads = jnp.where(lane >= 96, heads, 0.0).T.astype(BF16)

        def spread_out(k, carry, low=low, heads=heads):
            weights = wg1[k].reshape(256, D - CUT)[:, 1152 - CUT : D - CUT]
            outp[k, :, low : low + 128] = dot(weights, heads).astype(BF16)
            return carry

        lax.fori_loop(0, 8, spread_out, 0)
        for t in range(13):
            total = None
            for m in range(128 * t // 208, (128 * t + 127) // 208 + 1):
                term = dot(strip_pick(128 * t - 208 * m, 128, relative), outp[m, :, low : low + 128])
                total = term if total is None else total + term
            summed[low : low + 128, 128 * t : 128 * t + 128] = total.T.astype(BF16)
        for d in (2, 1, 3):
            go(sum_copy(half_rows, d))
            pl.when((x + d) % NX == 0)(tail_copy(half_rows, d).start)

    real = (lane < QW) | tail
    own = jnp.concatenate([summed[:, quarter(x)], summed[:, 4 * QW : D]], axis=1).astype(F32)
    base = jnp.concatenate([images[:, quarter(x)], images[:, 4 * QW : D]], axis=1).astype(F32)
    for h in range(2):
        for d in (1, 3, 2):
            sum_copy(h, d).wait_recv()
            pl.when(tail)(tail_copy(h, d).wait_recv)

    attn = own
    for d in (1, 2, 3):
        attn += jnp.concatenate([landed[0, d - 1], landed[1, d - 1]], axis=0).astype(F32)
    residual = jnp.where(real, base + attn, 0.0)

    routed = jnp.where(real, residual - image_mean, 0.0).astype(BF16)
    chosen = dot(choosing, routed, ((0,), (0,)))

    def folded(value):
        return jnp.concatenate([value[:, 0:256].reshape(32, 8, 256), value[:, 256:512].reshape(32, 8, 256)], axis=1).astype(BF16)

    def unfolded(value):
        value = value.reshape(32, 16, 256).astype(F32)
        return value[:, 0:8].reshape(256, 256).astype(BF16), value[:, 8:16].reshape(256, 256).astype(BF16)

    picked[...] = folded(chosen)

    def a_copy(i, d):
        to_y, to_z = (y + 2 * i) % NY, (z + d) % NZ
        return remote(
            picked.at[4 * to_z + to_y // 2], arrived.at[pair, z], a_send.at[i, d], a_recv.at[i, d], device(x, to_y, to_z, c)
        )

    for i, d in FAR:
        a_copy(i, d).start()
    arrived[pair, z] = picked[4 * z + pair]

    class Both:
        def __init__(self, main, extra, is_tail):
            self.main, self.extra, self.is_tail = main, extra, is_tail

        def start(self):
            self.main.start()
            pl.when(self.is_tail)(self.extra.start)

        def wait_send(self):
            self.main.wait_send()
            pl.when(self.is_tail)(self.extra.wait_send)

        def wait_recv(self):
            self.main.wait_recv()
            pl.when(self.is_tail)(self.extra.wait_recv)

    def pieces(src_main, dst_main, src_extra, dst_extra, send, recv, target, is_tail):
        return Both(
            remote(src_main, dst_main, send.at[0], recv.at[0], target),
            remote(src_extra, dst_extra, send.at[1], recv.at[1], target),
            is_tail,
        )

    for i, d in FAR[::-1]:
        a_copy(i, d).wait_recv()
    left, right = unfolded(arrived[...])
    rows[par, c, :, quarter(x)] = jnp.concatenate([left, right[:, 0:128]], axis=1)

    @pl.when(tail)
    def _():
        rows[par, c, :, 4 * QW : D] = right[:, 128:256]

    def same(parity, q_index, low, high, send, recv, target):
        main = rows.at[parity, c, low:high, quarter(q_index)]
        extra = rows.at[parity, c, low:high, 4 * QW : D]
        return pieces(main, main, extra, extra, send, recv, target, q_index == 0)

    def cut(which, j):
        return ((0, 128), (128, 256))[j] if which == 0 else ((0, 64), (64, 128))[j]

    def x_piece(which, way, j, q_index):
        low, high = cut(which, way if j == 2 else j)
        return same(
            par if which == 0 else 1 - par, q_index, low, high,
            xg_send.at[which, way, j], xg_recv.at[which, way, j], xdev(1 if way == 0 else 3),
        )

    def x_from(way, j):
        hops = 2 if j == 2 else 1
        return (x + NX - hops) % NX if way == 0 else (x + hops) % NX

    def y_piece(j, parity):
        low, high = (0, 128) if j == 0 else (128, 256)
        q_index = (x + (0, 0, NX - 1, 1, 2)[j]) % NX
        return same(parity, q_index, low, high, yp_send.at[j], yp_recv.at[j], mate)

    group_sent, to_core = [], ([], [])

    def put(copy):
        copy.start()
        group_sent.append(copy)

    def over(which, q_index, low, high):
        index = len(to_core[0]) + len(to_core[1])
        copy = same(par if which == 0 else 1 - par, q_index, low, high, cg_send.at[index], cg_recv.at[index], core)
        put(copy)
        to_core[which].append(copy)

    def take_x(which, way, j):
        q_index = x_from(way, j)
        x_piece(which, way, j, q_index).wait_recv()
        if j == way:
            put(x_piece(which, way, 2, q_index))
        if which == 0 and (way, j) in ((0, 1), (1, 1), (1, 2)):
            put(y_piece({(0, 1): 2, (1, 1): 3, (1, 2): 4}[way, j], par))
        over(which, q_index, *cut(which, way if j == 2 else j))

    def send_x(which):
        for way, j in ((0, 0), (1, 1), (0, 1), (1, 0)):
            put(x_piece(which, way, j, x))

    def take_y(j):
        y_piece(j, 1 - par).wait_recv()
        if j == 0:
            send_x(1)
        over(1, (x + (0, 0, NX - 1, 1, 2)[j]) % NX, *((0, 128) if j == 0 else (128, 256)))

    send_x(0)
    put(y_piece(0, par))
    put(y_piece(1, par))
    over(0, x, 0, 256)

    def expert(parity, core_index):
        values = rows[parity, core_index].astype(F32)
        center = values - jnp.mean(values, axis=-1, keepdims=True)
        spread = jnp.mean(center * center, axis=-1, keepdims=True)
        normed = (center * lax.rsqrt(spread + 1e-06) * mlp_gain[...].reshape(1, D)).astype(BF16)
        hidden = gelu_tanh(dot(normed, w_in[...])).astype(BF16)
        parts[parity, core_index] = dot(hidden, w_out[...]).astype(BF16)

    def r1_copy(k):
        parity = par if k == 0 else 1 - par
        return remote(parts.at[parity, 1 - c], r1.at[parity], r1_send.at[k], r1_recv.at[k], core)

    take_x(0, 0, 0)
    take_x(0, 1, 1)
    take_y(0)
    take_x(0, 0, 1)
    take_x(0, 1, 0)
    take_y(1)
    take_x(0, 0, 2)
    take_x(0, 1, 2)
    take_x(1, 0, 0)
    take_x(1, 1, 1)
    for load in loads[9:]:
        load.wait()
    for copy in to_core[0]:
        copy.wait_recv()
    expert(par, 1 - c)
    r1_copy(0).start()
    take_x(1, 0, 1)
    take_x(1, 1, 0)
    take_y(3)
    take_y(2)
    expert(par, c)
    take_x(1, 0, 2)
    take_x(1, 1, 2)
    take_y(4)
    def both_cores(parity):
        q[parity] = (parts[parity, c].astype(F32) + r1[parity].astype(F32)).astype(BF16)

    def quarters(src, rows_of, rows_to, dst, send, recv, d):
        to = (x + d) % NX
        return pieces(
            src.at[rows_of, quarter(to)], dst.at[d - 1, rows_to, 0:QW], src.at[rows_of, 4 * QW : D], dst.at[d - 1, rows_to, QW:QP],
            send.at[d - 1], recv.at[d - 1], xdev(d), to == 0,
        )

    def got(copy):
        copy.main.wait_recv()
        pl.when(tail)(copy.extra.wait_recv)

    def own_sum_copy(d):
        return quarters(q.at[par], pl.ds(0, FIRST), pl.ds(0, FIRST), r2a, r2_send, r2_recv, d)

    def mate_sum_copy(i, d):
        part = pl.ds(i * HALF, HALF)
        return quarters(q.at[1 - par], part, part, r2c, r2c_send.at[i], r2c_recv.at[i], d)

    def rest_copy():
        return remote(q.at[1 - par, FIRST:256], r2b, r2y_send, r2y_recv, mate)

    def late_copy(d):
        return quarters(sb, pl.ds(0, 256 - FIRST), pl.ds(0, 256 - FIRST), r3b, r3_send, r3_recv, d)

    def summed_copy(i):
        part = pl.ds(i * HALF, HALF)
        return remote(sa.at[part], r3a.at[part], r3y_send.at[i], r3y_recv.at[i], mate)

    def mine_of(value):
        return jnp.concatenate([value[:, quarter(x)], value[:, 4 * QW : D]], axis=1).astype(F32)

    r1_copy(0).wait_recv()
    both_cores(par)
    for d in (2, 1, 3):
        own_sum_copy(d).start()
    for copy in to_core[1]:
        copy.wait_recv()
    expert(1 - par, 1 - c)
    r1_copy(1).start()
    expert(1 - par, c)
    r1_copy(1).wait_recv()
    both_cores(1 - par)
    rest_copy().start()
    for i in range(2):
        for d in (2, 1, 3):
            mate_sum_copy(i, d).start()
    for d in (1, 3, 2):
        got(own_sum_copy(d))
    own_total = mine_of(q.at[par, 0:FIRST])
    for d in (1, 2, 3):
        own_total += r2a[d - 1].astype(F32)

    def pass_on(i):
        for d in (1, 3, 2):
            got(mate_sum_copy(i, d))
        low, high = i * HALF, (i + 1) * HALF
        total = mine_of(q.at[1 - par, low:high])
        for d in (1, 2, 3):
            total += r2c[d - 1, low:high].astype(F32)
        sa[low:high] = jnp.where(real, total, 0.0).astype(BF16)
        summed_copy(i).start()

    pass_on(0)
    rest_copy().wait_recv()
    sb[...] = (q[par, FIRST:256].astype(F32) + r2b[...].astype(F32)).astype(BF16)
    for d in (2, 1, 3):
        late_copy(d).start()
    pass_on(1)
    total = mine_of(sb)
    summed_copy(0).wait_recv()
    summed_copy(1).wait_recv()
    high_rows = jnp.where(real, own_total + r3a[...].astype(F32), 0.0)
    for d in (1, 3, 2):
        got(late_copy(d))
        total += r3b[d - 1].astype(F32)
    result = jnp.concatenate([high_rows, jnp.where(real, total, 0.0)], axis=0)

    returning[...] = folded(result).reshape(4, 8, 16, 256)

    def aa_copy(i, d):
        to_y, to_z = (y + 2 * i) % NY, (z + d) % NZ
        return remote(
            returning.at[to_y // 2, to_z], home.at[4 * z + pair], aa_send.at[i, d], aa_recv.at[i, d], device(x, to_y, to_z, c)
        )

    for i, d in FAR:
        aa_copy(i, d).start()
    home[4 * z + pair] = returning[pair, z]
    for i, d in FAR[::-1]:
        aa_copy(i, d).wait_recv()
    left, right = unfolded(home[...])
    final[...] = (residual + jnp.concatenate([dot(placing, left), dot(placing, right)], axis=1)).astype(BF16)

    def f_copy(d):
        to = pl.ds(pl.multiple_of((x + d) % NX * 64, 64), 64)
        return pieces(
            final.at[to, 0:QW], gathered.at[:, quarter(x)],
            final.at[to, QW:QP], gathered.at[:, 4 * QW : D],
            f_send.at[d - 1], f_recv.at[d - 1], xdev(d), tail,
        )

    for d in (2, 1, 3):
        f_copy(d).start()
    mine = pl.ds(pl.multiple_of(x * 64, 64), 64)
    gathered[:, quarter(x)] = final[mine, 0:QW]

    @pl.when(tail)
    def _():
        gathered[:, 4 * QW : D] = final[mine, QW:QP]

    for d in (1, 3, 2):
        copy = f_copy(d)
        copy.main.wait_recv()
        pl.when((x + NX - d) % NX == 0)(copy.extra.wait_recv)
    out[...] = gathered[...]

    for copy in started:
        copy.wait_send()
    for h in range(2):
        for d in (1, 2, 3):
            pl.when((x + d) % NX == 0)(tail_copy(h, d).wait_send)
    for i, d in FAR:
        a_copy(i, d).wait_send()
        aa_copy(i, d).wait_send()
    for copy in group_sent:
        copy.wait_send()
    for k in range(2):
        r1_copy(k).wait_send()
    for d in (1, 2, 3):
        own_sum_copy(d).wait_send()
        mate_sum_copy(0, d).wait_send()
        mate_sum_copy(1, d).wait_send()
        late_copy(d).wait_send()
        f_copy(d).wait_send()
    rest_copy().wait_send()
    summed_copy(0).wait_send()
    summed_copy(1).wait_send()


def block(images, attn_gain, mlp_gain, qkv, proj_t, ids_t, gates_t, kept, counts, w_in, w_out):
    sem = pltpu.SemaphoreType.DMA
    vm = pl.BlockSpec(memory_space=pltpu.VMEM)
    hbm = pl.BlockSpec(memory_space=pl.ANY)

    def v(*shape, kind=BF16):
        return pltpu.VMEM(shape, kind)

    return pl.pallas_call(
        block_kernel,
        name="block",
        out_shape=jax.ShapeDtypeStruct((64, D), BF16),
        in_specs=[hbm] * 11,
        out_specs=vm,
        scratch_shapes=[
            v(PATCHES, D), v(D, kind=F32), v(D, kind=F32), v(3, STRIP, 416), v(STRIP, 416),
            v(2, PATCHES, kind=jnp.int32), v(2, PATCHES), v(8, EXPERTS, kind=jnp.int32), v(1, EXPERTS, kind=jnp.int32),
            v(8, NY, 2, ROWS, CUT), v(NZ, 8, 2, ROWS, D - CUT), v(4, ROWS, D, kind=F32),
            v(8, PATCHES, 256), v(8, PATCHES, 256), v(PATCHES, 1280, kind=F32), v(8, PATCHES, 256), v(PATCHES, D),
            v(2, 3, 128, QP),
            v(D, 512), v(512, D), v(32, 16, 256), v(4, 8, 16, 256), v(2, 2, 256, D), v(2, 2, 256, D), v(2, 256, D),
            v(2, 256, D), v(3, FIRST, QP), v(3, FIRST, QP), v(256 - FIRST, D), v(FIRST, QP), v(256 - FIRST, D), v(FIRST, QP), v(3, 256 - FIRST, QP),
            v(4, 8, 16, 256), v(32, 16, 256), v(256, QP), v(64, D),
            sem((2, 7)), sem((2, 7)), sem((2, 2, 20)), sem((2, 2, 20)), sem((2, 40)), sem((2, 40)),
            sem((2, 3)), sem((2, 3)), sem((2, 3)), sem((2, 3)),
            sem((11,)), sem((4, 8)), sem((4, 8)), sem((5, 2)), sem((5, 2)),
            sem((2, 2, 3, 2)), sem((2, 2, 3, 2)), sem((18, 2)), sem((18, 2)),
            sem((2,)), sem((2,)), sem((3, 2)), sem((3, 2)), sem((2, 3, 2)), sem((2, 3, 2)), sem, sem, sem((3, 2)), sem((3, 2)), sem((2,)), sem((2,)),
            sem((4, 8)), sem((4, 8)), sem((3, 2)), sem((3, 2)),
        ],
        compiler_params=pltpu.CompilerParams(collective_id=1, has_side_effects=True, vmem_limit_bytes=56 << 20),
    )(images, attn_gain, mlp_gain, qkv, proj_t, ids_t, gates_t, kept, counts, w_in, w_out)


def on_device(
    images, attn_gain, qkv_weight, proj_weight, mlp_gain, expert_in, expert_out,
    gate_values, expert_ids, kept_patches, kept_counts,
):
    return block(
        images, attn_gain, mlp_gain, qkv_weight, proj_weight.T, expert_ids.T, gate_values.T,
        kept_patches[0].T, kept_counts, expert_in, expert_out,
    )


def solution(mesh):
    placed = (
        P("dp", None), P(), P(None, "dp", "mp"), P("mp", "dp"), P(), P(None, ("dp", "mp")), P(("dp", "mp"), None),
        P("dp", None), P("dp", None), P("dp", None, None), P("dp", None),
    )
    return jax.shard_map(on_device, mesh=mesh, in_specs=placed, out_specs=P(("dp", "mp"), None), check_vma=False)
```

```python
import functools

import jax
import jax.numpy as jnp
from jax import lax
from jax.experimental import pallas as pl
from jax.experimental.pallas import tpu as pltpu
from jax.sharding import PartitionSpec as P

MESH = pl.DeviceIdType.MESH
EXPERTS = 32
PATCHES = 256
HEAD_DIM = 104
HEADS_HERE = 4
D = 1664
NX, NY, NZ = 4, 8, 8
STRIP = 13
ROWS = 16
QW = 384
QP = 512
F32 = jnp.float32
BF16 = jnp.bfloat16


def place():
    dp = lax.axis_index("dp")
    return lax.axis_index("mp"), (dp // 2) % NY, dp // (2 * NY), dp % 2


def device(x, y, z, c):
    return ((z * NY + y) * 2 + c, x)


def remote(src, dst, send, recv, target):
    return pltpu.make_async_remote_copy(
        src_ref=src, dst_ref=dst, send_sem=send, recv_sem=recv, device_id=target, device_id_type=MESH
    )


def greet(partners):
    barrier = pltpu.get_barrier_semaphore()
    for partner in partners:
        pl.semaphore_signal(barrier, inc=1, device_id=partner, device_id_type=MESH)
    pl.semaphore_wait(barrier, len(partners))


def gelu_tanh(values):
    return 0.5 * values * (1.0 + jnp.tanh(0.7978845608028654 * (values + 0.044715 * values * values * values)))


def dot(a, b, dims=((1,), (0,))):
    return lax.dot_general(a, b, (dims, ((), ())), preferred_element_type=F32)


FAR = sorted(((i, d) for i in range(4) for d in range(8) if (i, d) != (0, 0)), key=lambda s: -(min(2 * s[0], 8 - 2 * s[0]) + min(s[1], 8 - s[1])))
FIRST = 160
HALF = FIRST // 2
CUT = 896
OFFSETS = (0, 1, -1, 2, -2, 3, -3, 4)
CHUNKS = ((0, 1), (1, 3), (3, 5), (5, 7), (7, 8))
ROUTE = (
    ("start", 0), ("first", 1), ("first", 2), ("start", 1), (1, 1, 0), (0, 1, 0), ("first", 3), ("first", 4), ("start", 2),
    (1, 1, 1), (0, 1, 1), (1, 2, 0), (0, 2, 0), ("first", 5), ("first", 6), ("start", 3), (1, 1, 2), (0, 1, 2), (1, 2, 1),
    (0, 2, 1), (1, 3, 0), (0, 3, 0), ("first", 7), ("start", 4), (0, 1, 3), (1, 1, 3), (0, 2, 2), (1, 2, 2), (0, 3, 1),
    (1, 3, 1), (0, 1, 4), (1, 4, 0), (1, 1, 4), (0, 2, 3), (1, 2, 3), (0, 3, 2), (0, 2, 4), (1, 3, 2), (0, 3, 3), (1, 4, 1),
    (1, 2, 4), (0, 3, 4), (1, 3, 3), (1, 4, 2), (0, 4, 3), (1, 3, 4), (0, 4, 4),
)


def slot_offset(s):
    return jnp.where(s % 2 == 1, (s + 1) // 2, -(s // 2))


def block_kernel(
    images_hbm, attn_gain_hbm, mlp_gain_hbm, qkv_hbm, proj_hbm, ids_hbm, gates_hbm, kept_hbm, counts_hbm,
    w_in_hbm, w_out_hbm, out,
    images, attn_gain, mlp_gain, qkv, proj, ids_t, gates_t, kept, counts,
    wg0, wg1, scratch_strip, exp0, exp1, acc, outp, summed, landed,
    w_in, w_out, picked, arrived, rows, parts, r1, q, r2a, r2c, r2b, sa, sb, r3a, r3b, returning, home, final, gathered,
    s1_send, s1_recv, ring_send, ring_recv, core_send, core_recv, x_send, x_recv, t_send, t_recv,
    w_sem, a_send, a_recv, yp_send, yp_recv, xg_send, xg_recv, cg_send, cg_recv,
    r1_send, r1_recv, r2_send, r2_recv, r2c_send, r2c_recv, r2y_send, r2y_recv, r3_send, r3_recv, r3y_send, r3y_recv,
    aa_send, aa_recv, f_send, f_recv,
):
    x, y, z, c = place()
    par, pair = y % 2, y // 2
    tail = x == 0

    def xdev(d):
        return device((x + d) % NX, y, z, c)

    def ydev(d):
        return device(x, (y + d) % NY, z, c)

    def zdev(d):
        return device(x, y, (z + d) % NZ, c)

    core = device(x, y, z, 1 - c)
    mate = device(x, y + 1 - 2 * par, z, c)

    def quarter(k):
        return pl.ds(pl.multiple_of(k * QW, 128), QW)

    near = [ydev(1), ydev(NY - 1), zdev(1), zdev(NZ - 1), core, xdev(1), xdev(3), xdev(2)]
    barrier = pltpu.get_barrier_semaphore()
    for partner in near:
        pl.semaphore_signal(barrier, inc=1, device_id=partner, device_id_type=MESH)
    arguments = (
        (qkv_hbm, qkv), (proj_hbm, proj), (kept_hbm, kept), (counts_hbm, counts), (ids_hbm, ids_t), (gates_hbm, gates_t),
        (images_hbm, images), (attn_gain_hbm, attn_gain), (mlp_gain_hbm, mlp_gain), (w_in_hbm, w_in), (w_out_hbm, w_out),
    )
    loads = [pltpu.make_async_copy(src, dst, w_sem.at[i]) for i, (src, dst) in enumerate(arguments)]
    for load in loads:
        load.start()
    for load in loads[0:6]:
        load.wait()

    scratch_strip[...] = jnp.zeros_like(scratch_strip)
    for i in range(3):
        scratch_strip[i, 0:STRIP, 0:416] = qkv[i].astype(F32)
    scratch_strip[3, 0:STRIP, 0:416] = proj[...].astype(F32)
    strip = scratch_strip[0]
    for i in range(1, 4):
        strip += pltpu.roll(scratch_strip[i], 416 * i, 1)
    strip = strip.astype(BF16)
    wg0[0, y, c] = strip[:, 0:CUT]
    wg1[z, 0, c] = strip[:, CUT:D]

    slot_col = lax.broadcasted_iota(jnp.int32, (256, 32), 0)
    expert_col = lax.broadcasted_iota(jnp.int32, (256, 32), 1)
    of_expert = jnp.where((slot_col >> 3) == expert_col, 1.0, 0.0)
    patch8 = dot(of_expert.astype(BF16), kept[...].astype(F32).astype(BF16), ((1,), (1,)))
    which = (lax.broadcasted_iota(jnp.int32, (256, 8), 0) & 7) == lax.broadcasted_iota(jnp.int32, (256, 8), 1)
    patch = jnp.sum(jnp.where(which, patch8, 0.0), axis=1, keepdims=True)
    valid = jnp.sum(of_expert * counts[...].astype(F32), axis=1, keepdims=True)
    lane128 = lax.broadcasted_iota(jnp.int32, (1, 128), 1)
    slot_rows = jnp.where(lane128 == 0, patch, jnp.where(lane128 == 1, valid, 0.0)).T
    row128 = lax.broadcasted_iota(jnp.int32, (128, 256), 0)
    meta = jnp.where(row128 == 0, ids_t[0:1, :].astype(F32), 0.0)
    meta = jnp.where(row128 == 1, ids_t[1:2, :].astype(F32), meta)
    meta = jnp.where(row128 == 2, gates_t[0:1, :].astype(F32), meta)
    meta = jnp.where(row128 == 3, gates_t[1:2, :].astype(F32), meta).T
    token = lax.broadcasted_iota(jnp.int32, (PATCHES, 256), 0)
    holds = token == slot_rows[0:1, :].astype(jnp.int32)
    slot_lane = lax.broadcasted_iota(jnp.int32, (1, 256), 1)
    slot_expert = (slot_lane >> 3).astype(F32)
    usable = (slot_lane & 7).astype(F32) < slot_rows[1:2, :]
    gate = jnp.where(meta[:, 0:1] == slot_expert, meta[:, 2:3], 0.0)
    gate += jnp.where(meta[:, 1:2] == slot_expert, meta[:, 3:4], 0.0)
    placing = jnp.where(holds & usable, gate, 0.0).astype(BF16)
    choosing = jnp.where(holds, 1.0, 0.0).astype(BF16)

    acc[...] = jnp.zeros_like(acc)
    pl.semaphore_wait(barrier, len(near))

    def ring(half, stage, sign):
        along_z = (half == 0) == (stage == 1)
        return zdev(sign + NZ) if along_z else ydev(sign + NY)

    def first_copy(half, slot):
        source = 0 if slot < 3 else slot - 2
        if half == 0:
            src, dst = wg0.at[source, y, c], wg0.at[slot, y, c]
        else:
            src, dst = wg1.at[z, source, c], wg1.at[z, slot, c]
        return remote(
            src, dst, s1_send.at[half], s1_recv.at[half, slot - 1], ring(half, 1, -1 if slot % 2 else 1)
        )

    def chunk_ref(half, pos, k):
        low, high = CHUNKS[k]
        if half == 0:
            return wg0.at[low:high, pos % NY, c]
        return wg1.at[pos % NZ, low:high, c]

    def here(half):
        return y if half == 0 else z

    def ring_copy(half, way, step, k):
        pos = here(half) - (step - 1) if way == 0 else here(half) + (step - 1)
        piece = chunk_ref(half, pos + 8, k)
        index = (step - 1) * 5 + k
        return remote(
            piece, piece, ring_send.at[half], ring_recv.at[half, way, index], ring(half, 2, 1 if way == 0 else -1)
        )

    def core_copy_w(half, pos, k):
        piece = chunk_ref(half, pos + 8, k)
        return remote(piece, piece, core_send.at[half], core_recv.at[half, k], core)

    def share(half, pos, k):
        core_copy_w(half, pos, k).start()

    started = []

    def go(copy):
        copy.start()
        started.append(copy)

    def begin(k):
        for half in range(2):
            for way in range(2):
                ring_copy(half, way, 1, k).start()
        for half in range(2):
            share(half, here(half), k)

    def last_way(k):
        return 1 if k < 3 else 0

    def advance(way, step, k):
        for half in range(2):
            ring_copy(half, way, step, k).wait_recv()
            if step < 3 or (step == 3 and way == last_way(k)):
                ring_copy(half, way, step + 1, k).start()
            share(half, here(half) - step if way == 0 else here(half) + step, k)

    col = lax.broadcasted_iota(jnp.int32, (1, 256), 1)
    inner = col & (ROWS - 1)
    own_slot = col >> 5
    absolute = jnp.where(inner < STRIP, STRIP * (col >> 4) + inner, -4096)
    turned = ((y + NY + slot_offset(own_slot)) % NY) * 2 + ((col >> 4) & 1)
    relative = jnp.where(inner < STRIP, STRIP * turned + inner, -4096)

    def strip_pick(first, count, target):
        feature = lax.broadcasted_iota(jnp.int32, (count, 256), 0) + first
        return jnp.where(feature == target, 1.0, 0.0).astype(BF16)

    def expand(m):
        low = (208 * m) // 128 * 128
        wide = min(384, D - low)
        exp0[m] = dot(normed[:, low : low + wide], strip_pick(low - 208 * m, wide, absolute)).astype(BF16)
        exp1[m] = dot(normed[:, low : low + wide], strip_pick(low - 208 * m, wide, relative)).astype(BF16)

    def project(k):
        acc[:, 0:CUT] += dot(exp0[(z + NZ + OFFSETS[k]) % NZ], wg0[k].reshape(256, CUT))

    def finish(k):
        low, high = CHUNKS[k]
        for half, piece in enumerate((wg0.at[low:high, :, c], wg1.at[:, low:high, c])):
            remote(piece, piece, core_send.at[half], core_recv.at[half, k], core).wait_recv()
        for slot in range(*CHUNKS[k]):
            project(slot)

    for half in range(2):
        first_copy(half, 1).start()
        first_copy(half, 2).start()
    for at, entry in enumerate(ROUTE):
        if entry[0] == "start":
            begin(entry[1])
        elif entry[0] == "first":
            for half in range(2):
                first_copy(half, entry[1]).wait_recv()
                if entry[1] <= 5:
                    first_copy(half, entry[1] + 2).start()
        else:
            advance(*entry)
        if at == 0:
            for load in loads[6:9]:
                load.wait()
            values = images[...].astype(F32)
            image_mean = jnp.mean(values, axis=-1, keepdims=True)
            center = values - image_mean
            spread = jnp.mean(center * center, axis=-1, keepdims=True)
            normed = (center * lax.rsqrt(spread + 1e-06) * attn_gain[...].reshape(1, D)).astype(BF16)
        if 8 <= at < 24 and at % 2 == 0:
            expand((at - 8) // 2)
        if at in (38, 42, 45):
            finish((38, 42, 45).index(at))
    finish(3)
    finish(4)
    for k in range(8):
        part = dot(exp1[k], wg1[k].reshape(256, D - CUT)[:, 0 : 1280 - CUT])
        late = part if k == 0 else late + part
    acc[:, CUT:1280] = late
    lane = lax.broadcasted_iota(jnp.int32, (1, QP), 1)
    keys = acc[:, 384:896].astype(BF16).astype(F32)
    keys = jnp.where((lane >= 32) & (lane < 448), keys, 0.0).T.astype(BF16)
    vals = acc[:, 768:1280].astype(BF16).astype(F32)

    def sum_copy(h, d):
        return remote(
            summed.at[128 * h : 128 * h + 128, quarter((x + d) % NX)], landed.at[h, d - 1, :, 0:QW],
            x_send.at[h, d - 1], x_recv.at[h, d - 1], xdev(d),
        )

    def tail_copy(h, d):
        return remote(
            summed.at[128 * h : 128 * h + 128, 4 * QW : D], landed.at[h, d - 1, :, QW:QP],
            t_send.at[h, d - 1], t_recv.at[h, d - 1], xdev(d),
        )

    for half_rows in range(2):
        low = 128 * half_rows
        query = pltpu.roll(acc[low : low + 128, 0:512].astype(BF16).astype(F32), 32, 1)
        mixed = jnp.zeros((128, QP), F32)
        for h in range(HEADS_HERE):
            in_q = (lane >= 32 + HEAD_DIM * h) & (lane < 32 + HEAD_DIM * (h + 1))
            in_v = (lane >= 64 + HEAD_DIM * h) & (lane < 64 + HEAD_DIM * (h + 1))
            scores = dot(jnp.where(in_q, query, 0.0).astype(BF16), keys) * HEAD_DIM ** (-0.5)
            top = jnp.max(scores, axis=-1, keepdims=True)
            grown = jnp.exp(scores - top)
            probs = (grown / jnp.sum(grown, axis=-1, keepdims=True)).astype(BF16)
            mixed += dot(probs, jnp.where(in_v, vals, 0.0).astype(BF16))
        heads = pltpu.roll(mixed.astype(BF16).astype(F32), 32, 1)
        heads = jnp.where(lane >= 96, heads, 0.0).T.astype(BF16)

        def spread_out(k, carry, low=low, heads=heads):
            weights = wg1[k].reshape(256, D - CUT)[:, 1152 - CUT : D - CUT]
            outp[k, :, low : low + 128] = dot(weights, heads).astype(BF16)
            return carry

        lax.fori_loop(0, 8, spread_out, 0)
        for t in range(13):
            total = None
            for m in range(128 * t // 208, (128 * t + 127) // 208 + 1):
                term = dot(strip_pick(128 * t - 208 * m, 128, relative), outp[m, :, low : low + 128])
                total = term if total is None else total + term
            summed[low : low + 128, 128 * t : 128 * t + 128] = total.T.astype(BF16)
        for d in (2, 1, 3):
            go(sum_copy(half_rows, d))
            pl.when((x + d) % NX == 0)(tail_copy(half_rows, d).start)

    real = (lane < QW) | tail
    own = jnp.concatenate([summed[:, quarter(x)], summed[:, 4 * QW : D]], axis=1).astype(F32)
    base = jnp.concatenate([images[:, quarter(x)], images[:, 4 * QW : D]], axis=1).astype(F32)
    for h in range(2):
        for d in (1, 3, 2):
            sum_copy(h, d).wait_recv()
            pl.when(tail)(tail_copy(h, d).wait_recv)

    attn = own
    for d in (1, 2, 3):
        attn += jnp.concatenate([landed[0, d - 1], landed[1, d - 1]], axis=0).astype(F32)
    residual = jnp.where(real, base + attn, 0.0)

    routed = jnp.where(real, residual - image_mean, 0.0).astype(BF16)
    chosen = dot(choosing, routed, ((0,), (0,)))

    def folded(value):
        return jnp.concatenate([value[:, 0:256].reshape(32, 8, 256), value[:, 256:512].reshape(32, 8, 256)], axis=1).astype(BF16)

    def unfolded(value):
        value = value.reshape(32, 16, 256).astype(F32)
        return value[:, 0:8].reshape(256, 256).astype(BF16), value[:, 8:16].reshape(256, 256).astype(BF16)

    picked[...] = folded(chosen)

    def a_copy(i, d):
        to_y, to_z = (y + 2 * i) % NY, (z + d) % NZ
        return remote(
            picked.at[4 * to_z + to_y // 2], arrived.at[pair, z], a_send, a_recv, device(x, to_y, to_z, c)
        )

    for i, d in FAR:
        a_copy(i, d).start()
    arrived[pair, z] = picked[4 * z + pair]

    class Both:
        def __init__(self, main, extra, is_tail):
            self.main, self.extra, self.is_tail = main, extra, is_tail

        def start(self):
            self.main.start()
            pl.when(self.is_tail)(self.extra.start)

        def wait_send(self):
            self.main.wait_send()
            pl.when(self.is_tail)(self.extra.wait_send)

        def wait_recv(self):
            self.main.wait_recv()
            pl.when(self.is_tail)(self.extra.wait_recv)

    def pieces(src_main, dst_main, src_extra, dst_extra, send, recv, target, is_tail):
        return Both(
            remote(src_main, dst_main, send.at[0], recv.at[0], target),
            remote(src_extra, dst_extra, send.at[1], recv.at[1], target),
            is_tail,
        )

    def all_of(send, recv):
        return remote(picked.at[0:31], home.at[0:31], send, recv, core)

    all_of(a_send, a_recv).wait_recv()
    left, right = unfolded(arrived[...])
    rows[par, c, :, quarter(x)] = jnp.concatenate([left, right[:, 0:128]], axis=1)

    @pl.when(tail)
    def _():
        rows[par, c, :, 4 * QW : D] = right[:, 128:256]

    def same(parity, q_index, low, high, send, recv, target):
        main = rows.at[parity, c, low:high, quarter(q_index)]
        extra = rows.at[parity, c, low:high, 4 * QW : D]
        return pieces(main, main, extra, extra, send, recv, target, q_index == 0)

    def cut(which, j):
        return ((0, 128), (128, 256))[j] if which == 0 else ((0, 64), (64, 128))[j]

    def x_piece(which, way, j, q_index):
        low, high = cut(which, way if j == 2 else j)
        return same(
            par if which == 0 else 1 - par, q_index, low, high,
            xg_send.at[which, way, j], xg_recv.at[which, way, j], xdev(1 if way == 0 else 3),
        )

    def x_from(way, j):
        hops = 2 if j == 2 else 1
        return (x + NX - hops) % NX if way == 0 else (x + hops) % NX

    def y_piece(j, parity):
        low, high = (0, 128) if j == 0 else (128, 256)
        q_index = (x + (0, 0, NX - 1, 1, 2)[j]) % NX
        return same(parity, q_index, low, high, yp_send.at[j], yp_recv.at[j], mate)

    group_sent = []

    def to_core_all(main, extra, which):
        return pieces(main, main, extra, extra, cg_send, cg_recv.at[which], core, x >= 0)


    def put(copy):
        copy.start()
        group_sent.append(copy)

    def over(which, q_index, low, high):
        same(par if which == 0 else 1 - par, q_index, low, high, cg_send, cg_recv.at[which], core).start()

    def take_x(which, way, j):
        q_index = x_from(way, j)
        x_piece(which, way, j, q_index).wait_recv()
        if j == way:
            put(x_piece(which, way, 2, q_index))
        if which == 0 and (way, j) in ((0, 1), (1, 1), (1, 2)):
            put(y_piece({(0, 1): 2, (1, 1): 3, (1, 2): 4}[way, j], par))
        over(which, q_index, *cut(which, way if j == 2 else j))

    def send_x(which):
        for way, j in ((0, 0), (1, 1), (0, 1), (1, 0)):
            put(x_piece(which, way, j, x))

    def take_y(j):
        y_piece(j, 1 - par).wait_recv()
        if j == 0:
            send_x(1)
        over(1, (x + (0, 0, NX - 1, 1, 2)[j]) % NX, *((0, 128) if j == 0 else (128, 256)))

    send_x(0)
    put(y_piece(0, par))
    put(y_piece(1, par))
    over(0, x, 0, 256)

    def expert(parity, core_index):
        values = rows[parity, core_index].astype(F32)
        center = values - jnp.mean(values, axis=-1, keepdims=True)
        spread = jnp.mean(center * center, axis=-1, keepdims=True)
        normed = (center * lax.rsqrt(spread + 1e-06) * mlp_gain[...].reshape(1, D)).astype(BF16)
        hidden = gelu_tanh(dot(normed, w_in[...])).astype(BF16)
        parts[parity, core_index] = dot(hidden, w_out[...]).astype(BF16)

    def r1_copy(k):
        parity = par if k == 0 else 1 - par
        return remote(parts.at[parity, 1 - c], r1.at[parity], r1_send.at[k], r1_recv.at[k], core)

    take_x(0, 0, 0)
    take_x(0, 1, 1)
    take_y(0)
    take_x(0, 0, 1)
    take_x(0, 1, 0)
    take_y(1)
    take_x(0, 0, 2)
    take_x(0, 1, 2)
    take_x(1, 0, 0)
    take_x(1, 1, 1)
    for load in loads[9:]:
        load.wait()
    to_core_all(rows.at[:, :, :, 0:QW], rows.at[0, 0, :, 0:128], 0).wait_recv()
    expert(par, 1 - c)
    r1_copy(0).start()
    take_x(1, 0, 1)
    take_x(1, 1, 0)
    take_y(3)
    take_y(2)
    expert(par, c)
    take_x(1, 0, 2)
    take_x(1, 1, 2)
    take_y(4)
    def both_cores(parity):
        q[parity] = (parts[parity, c].astype(F32) + r1[parity].astype(F32)).astype(BF16)

    def quarters(src, rows_of, rows_to, dst, send, recv, d):
        to = (x + d) % NX
        return pieces(
            src.at[rows_of, quarter(to)], dst.at[d - 1, rows_to, 0:QW], src.at[rows_of, 4 * QW : D], dst.at[d - 1, rows_to, QW:QP],
            send.at[d - 1], recv.at[d - 1], xdev(d), to == 0,
        )

    def got(copy):
        copy.main.wait_recv()
        pl.when(tail)(copy.extra.wait_recv)

    def own_sum_copy(d):
        return quarters(q.at[par], pl.ds(0, FIRST), pl.ds(0, FIRST), r2a, r2_send, r2_recv, d)

    def mate_sum_copy(i, d):
        part = pl.ds(i * HALF, HALF)
        return quarters(q.at[1 - par], part, part, r2c, r2c_send.at[i], r2c_recv.at[i], d)

    def rest_copy():
        return remote(q.at[1 - par, FIRST:256], r2b, r2y_send, r2y_recv, mate)

    def late_copy(d):
        return quarters(sb, pl.ds(0, 256 - FIRST), pl.ds(0, 256 - FIRST), r3b, r3_send, r3_recv, d)

    def summed_copy(i):
        part = pl.ds(i * HALF, HALF)
        return remote(sa.at[part], r3a.at[part], r3y_send.at[i], r3y_recv.at[i], mate)

    def mine_of(value):
        return jnp.concatenate([value[:, quarter(x)], value[:, 4 * QW : D]], axis=1).astype(F32)

    r1_copy(0).wait_recv()
    both_cores(par)
    for d in (2, 1, 3):
        own_sum_copy(d).start()
    to_core_all(rows.at[:, :, :, 0:QW], rows.at[0, 0, :, 0:128], 1).wait_recv()
    expert(1 - par, 1 - c)
    r1_copy(1).start()
    expert(1 - par, c)
    r1_copy(1).wait_recv()
    both_cores(1 - par)
    rest_copy().start()
    for i in range(2):
        for d in (2, 1, 3):
            mate_sum_copy(i, d).start()
    for d in (1, 3, 2):
        got(own_sum_copy(d))
    own_total = mine_of(q.at[par, 0:FIRST])
    for d in (1, 2, 3):
        own_total += r2a[d - 1].astype(F32)

    def pass_on(i):
        for d in (1, 3, 2):
            got(mate_sum_copy(i, d))
        low, high = i * HALF, (i + 1) * HALF
        total = mine_of(q.at[1 - par, low:high])
        for d in (1, 2, 3):
            total += r2c[d - 1, low:high].astype(F32)
        sa[low:high] = jnp.where(real, total, 0.0).astype(BF16)
        summed_copy(i).start()

    pass_on(0)
    rest_copy().wait_recv()
    sb[...] = (q[par, FIRST:256].astype(F32) + r2b[...].astype(F32)).astype(BF16)
    for d in (2, 1, 3):
        late_copy(d).start()
    pass_on(1)
    total = mine_of(sb)
    summed_copy(0).wait_recv()
    summed_copy(1).wait_recv()
    high_rows = jnp.where(real, own_total + r3a[...].astype(F32), 0.0)
    for d in (1, 3, 2):
        got(late_copy(d))
        total += r3b[d - 1].astype(F32)
    result = jnp.concatenate([high_rows, jnp.where(real, total, 0.0)], axis=0)

    returning[...] = folded(result).reshape(4, 8, 16, 256)

    def aa_copy(i, d):
        to_y, to_z = (y + 2 * i) % NY, (z + d) % NZ
        return remote(
            returning.at[to_y // 2, to_z], home.at[4 * z + pair], aa_send, aa_recv, device(x, to_y, to_z, c)
        )

    for i, d in FAR:
        aa_copy(i, d).start()
    home[4 * z + pair] = returning[pair, z]
    all_of(aa_send, aa_recv).wait_recv()
    left, right = unfolded(home[...])
    final[...] = (residual + jnp.concatenate([dot(placing, left), dot(placing, right)], axis=1)).astype(BF16)

    def f_copy(d):
        to = pl.ds(pl.multiple_of((x + d) % NX * 64, 64), 64)
        return pieces(
            final.at[to, 0:QW], gathered.at[:, quarter(x)],
            final.at[to, QW:QP], gathered.at[:, 4 * QW : D],
            f_send.at[d - 1], f_recv.at[d - 1], xdev(d), tail,
        )

    for d in (2, 1, 3):
        f_copy(d).start()
    mine = pl.ds(pl.multiple_of(x * 64, 64), 64)
    gathered[:, quarter(x)] = final[mine, 0:QW]

    @pl.when(tail)
    def _():
        gathered[:, 4 * QW : D] = final[mine, QW:QP]

    for d in (1, 3, 2):
        copy = f_copy(d)
        copy.main.wait_recv()
        pl.when((x + NX - d) % NX == 0)(copy.extra.wait_recv)
    out[...] = gathered[...]

    for copy in started:
        copy.wait_send()
    for h in range(2):
        for d in (1, 2, 3):
            pl.when((x + d) % NX == 0)(tail_copy(h, d).wait_send)
    all_of(a_send, a_recv).wait_send()
    all_of(aa_send, aa_recv).wait_send()
    for half, (strips, ringed, shared) in enumerate(
        ((wg0.at[0:7, 0, 0], wg0.at[:, 0:7, 0], wg0.at[:, :, 0]), (wg1.at[0, 0:7, 0], wg1.at[0:7, :, 0], wg1.at[:, :, 0]))
    ):
        remote(strips, strips, s1_send.at[half], s1_recv.at[half, 0], core).wait_send()
        remote(ringed, ringed, ring_send.at[half], ring_recv.at[half, 0, 0], core).wait_send()
        remote(shared, shared, core_send.at[half], core_recv.at[half, 0], core).wait_send()
    to_core_all(rows.at[:, :, :, 0 : 2 * QW], rows.at[0, :, :, 0:128], 0).wait_send()
    for copy in group_sent:
        copy.wait_send()
    for k in range(2):
        r1_copy(k).wait_send()
    for d in (1, 2, 3):
        own_sum_copy(d).wait_send()
        mate_sum_copy(0, d).wait_send()
        mate_sum_copy(1, d).wait_send()
        late_copy(d).wait_send()
        f_copy(d).wait_send()
    rest_copy().wait_send()
    summed_copy(0).wait_send()
    summed_copy(1).wait_send()


def block(images, attn_gain, mlp_gain, qkv, proj_t, ids_t, gates_t, kept, counts, w_in, w_out):
    sem = pltpu.SemaphoreType.DMA
    vm = pl.BlockSpec(memory_space=pltpu.VMEM)
    hbm = pl.BlockSpec(memory_space=pl.ANY)

    def v(*shape, kind=BF16):
        return pltpu.VMEM(shape, kind)

    return pl.pallas_call(
        block_kernel,
        name="block",
        out_shape=jax.ShapeDtypeStruct((64, D), BF16),
        in_specs=[hbm] * 11,
        out_specs=vm,
        scratch_shapes=[
            v(PATCHES, D), v(D, kind=F32), v(D, kind=F32), v(3, STRIP, 416), v(STRIP, 416),
            v(2, PATCHES, kind=jnp.int32), v(2, PATCHES), v(8, EXPERTS, kind=jnp.int32), v(1, EXPERTS, kind=jnp.int32),
            v(8, NY, 2, ROWS, CUT), v(NZ, 8, 2, ROWS, D - CUT), v(4, ROWS, D, kind=F32),
            v(8, PATCHES, 256), v(8, PATCHES, 256), v(PATCHES, 1280, kind=F32), v(8, PATCHES, 256), v(PATCHES, D),
            v(2, 3, 128, QP),
            v(D, 512), v(512, D), v(32, 16, 256), v(4, 8, 16, 256), v(2, 2, 256, D), v(2, 2, 256, D), v(2, 256, D),
            v(2, 256, D), v(3, FIRST, QP), v(3, FIRST, QP), v(256 - FIRST, D), v(FIRST, QP), v(256 - FIRST, D), v(FIRST, QP), v(3, 256 - FIRST, QP),
            v(4, 8, 16, 256), v(32, 16, 256), v(256, QP), v(64, D),
            sem((2,)), sem((2, 7)), sem((2,)), sem((2, 2, 20)), sem((2,)), sem((2, 5)),
            sem((2, 3)), sem((2, 3)), sem((2, 3)), sem((2, 3)),
            sem((11,)), sem, sem, sem((5, 2)), sem((5, 2)),
            sem((2, 2, 3, 2)), sem((2, 2, 3, 2)), sem((2,)), sem((2, 2)),
            sem((2,)), sem((2,)), sem((3, 2)), sem((3, 2)), sem((2, 3, 2)), sem((2, 3, 2)), sem, sem, sem((3, 2)), sem((3, 2)), sem((2,)), sem((2,)),
            sem, sem, sem((3, 2)), sem((3, 2)),
        ],
        compiler_params=pltpu.CompilerParams(collective_id=1, has_side_effects=True, vmem_limit_bytes=56 << 20),
    )(images, attn_gain, mlp_gain, qkv, proj_t, ids_t, gates_t, kept, counts, w_in, w_out)


def on_device(
    images, attn_gain, qkv_weight, proj_weight, mlp_gain, expert_in, expert_out,
    gate_values, expert_ids, kept_patches, kept_counts,
):
    return block(
        images, attn_gain, mlp_gain, qkv_weight, proj_weight.T, expert_ids.T, gate_values.T,
        kept_patches[0].T, kept_counts, expert_in, expert_out,
    )


def solution(mesh):
    placed = (
        P("dp", None), P(), P(None, "dp", "mp"), P("mp", "dp"), P(), P(None, ("dp", "mp")), P(("dp", "mp"), None),
        P("dp", None), P("dp", None), P("dp", None, None), P("dp", None),
    )
    return jax.shard_map(on_device, mesh=mesh, in_specs=placed, out_specs=P(("dp", "mp"), None), check_vma=False)
```

```python
import functools

import jax
import jax.numpy as jnp
from jax import lax
from jax.experimental import pallas as pl
from jax.experimental.pallas import tpu as pltpu
from jax.sharding import PartitionSpec as P

MESH = pl.DeviceIdType.MESH
EXPERTS = 32
PATCHES = 256
HEAD_DIM = 104
HEADS_HERE = 4
D = 1664
NX, NY, NZ = 4, 8, 8
STRIP = 13
ROWS = 16
QW = 384
QP = 512
F32 = jnp.float32
BF16 = jnp.bfloat16


def place():
    dp = lax.axis_index("dp")
    return lax.axis_index("mp"), (dp // 2) % NY, dp // (2 * NY), dp % 2


def device(x, y, z, c):
    return ((z * NY + y) * 2 + c, x)


def remote(src, dst, send, recv, target):
    return pltpu.make_async_remote_copy(
        src_ref=src, dst_ref=dst, send_sem=send, recv_sem=recv, device_id=target, device_id_type=MESH
    )


def greet(partners):
    barrier = pltpu.get_barrier_semaphore()
    for partner in partners:
        pl.semaphore_signal(barrier, inc=1, device_id=partner, device_id_type=MESH)
    pl.semaphore_wait(barrier, len(partners))


def gelu_tanh(values):
    return 0.5 * values * (1.0 + jnp.tanh(0.7978845608028654 * (values + 0.044715 * values * values * values)))


def dot(a, b, dims=((1,), (0,))):
    return lax.dot_general(a, b, (dims, ((), ())), preferred_element_type=F32)


FAR = sorted(((i, d) for i in range(4) for d in range(8) if (i, d) != (0, 0)), key=lambda s: -(min(2 * s[0], 8 - 2 * s[0]) + min(s[1], 8 - s[1])))
FIRST = 160
HALF = FIRST // 2
CUT = 896
OFFSETS = (0, 1, -1, 2, -2, 3, -3, 4)
CHUNKS = ((0, 1), (1, 3), (3, 5), (5, 7), (7, 8))
ROUTE = (('start', 0), ('first', 1), ('first', 2), ('start', 1), (1, 1, 0), (0, 1, 0), ('first', 3), ('first', 4), ('start', 2), (1, 1, 1), (0, 1, 1), (1, 2, 0), (0, 2, 0), ('first', 5), ('first', 6), ('start', 3), (1, 1, 2), (0, 1, 2), (1, 2, 1), (0, 2, 1), (1, 3, 0), (0, 3, 0), ('first', 7), ('start', 4), (0, 1, 3), (1, 1, 3), (0, 2, 2), (1, 2, 2), (0, 3, 1), (1, 3, 1), (0, 4, 0), (0, 1, 4), (1, 1, 4), (0, 2, 3), (1, 2, 3), (0, 3, 2), (1, 3, 2), (0, 2, 4), (1, 4, 1), (1, 2, 4), (0, 3, 3), (1, 3, 3), (1, 4, 2), (0, 3, 4), (1, 3, 4), (0, 4, 3), (0, 4, 4))


def slot_offset(s):
    return jnp.where(s % 2 == 1, (s + 1) // 2, -(s // 2))


def block_kernel(
    images_hbm, attn_gain_hbm, mlp_gain_hbm, qkv_hbm, proj_hbm, ids_hbm, gates_hbm, kept_hbm, counts_hbm,
    w_in_hbm, w_out_hbm, out,
    images, attn_gain, mlp_gain, qkv, proj, ids_t, gates_t, kept, counts,
    wg0, wg1, scratch_strip, exp0, exp1, acc, outp, summed, landed,
    w_in, w_out, picked, arrived, rows, parts, r1, q, r2a, r2c, r2b, sa, sb, r3a, r3b, returning, home, final, gathered,
    s1_send, s1_recv, ring_send, ring_recv, core_send, core_recv, x_send, x_recv, t_send, t_recv,
    w_sem, a_send, a_recv, yp_send, yp_recv, xg_send, xg_recv, cg_send, cg_recv,
    r1_send, r1_recv, r2_send, r2_recv, r2c_send, r2c_recv, r2y_send, r2y_recv, r3_send, r3_recv, r3y_send, r3y_recv,
    aa_send, aa_recv, f_send, f_recv,
):
    x, y, z, c = place()
    par, pair = y % 2, y // 2
    tail = x == 0

    def xdev(d):
        return device((x + d) % NX, y, z, c)

    def ydev(d):
        return device(x, (y + d) % NY, z, c)

    def zdev(d):
        return device(x, y, (z + d) % NZ, c)

    core = device(x, y, z, 1 - c)
    mate = device(x, y + 1 - 2 * par, z, c)

    def quarter(k):
        return pl.ds(pl.multiple_of(k * QW, 128), QW)

    near = [ydev(1), ydev(NY - 1), zdev(1), zdev(NZ - 1), core, xdev(1), xdev(3), xdev(2)]
    barrier = pltpu.get_barrier_semaphore()
    for partner in near:
        pl.semaphore_signal(barrier, inc=1, device_id=partner, device_id_type=MESH)
    arguments = (
        (qkv_hbm, qkv), (proj_hbm, proj), (kept_hbm, kept), (counts_hbm, counts), (ids_hbm, ids_t), (gates_hbm, gates_t),
        (images_hbm, images), (attn_gain_hbm, attn_gain), (mlp_gain_hbm, mlp_gain), (w_in_hbm, w_in), (w_out_hbm, w_out),
    )
    loads = [pltpu.make_async_copy(src, dst, w_sem.at[i]) for i, (src, dst) in enumerate(arguments)]
    for load in loads:
        load.start()
    for load in loads[0:6]:
        load.wait()

    scratch_strip[...] = jnp.zeros_like(scratch_strip)
    for i in range(3):
        scratch_strip[i, 0:STRIP, 0:416] = qkv[i].astype(F32)
    scratch_strip[3, 0:STRIP, 0:416] = proj[...].astype(F32)
    strip = scratch_strip[0]
    for i in range(1, 4):
        strip += pltpu.roll(scratch_strip[i], 416 * i, 1)
    strip = strip.astype(BF16)
    wg0[0, y, c] = strip[:, 0:CUT]
    wg1[z, 0, c] = strip[:, CUT:D]

    slot_col = lax.broadcasted_iota(jnp.int32, (256, 32), 0)
    expert_col = lax.broadcasted_iota(jnp.int32, (256, 32), 1)
    of_expert = jnp.where((slot_col >> 3) == expert_col, 1.0, 0.0)
    patch8 = dot(of_expert.astype(BF16), kept[...].astype(F32).astype(BF16), ((1,), (1,)))
    which = (lax.broadcasted_iota(jnp.int32, (256, 8), 0) & 7) == lax.broadcasted_iota(jnp.int32, (256, 8), 1)
    patch = jnp.sum(jnp.where(which, patch8, 0.0), axis=1, keepdims=True)
    valid = jnp.sum(of_expert * counts[...].astype(F32), axis=1, keepdims=True)
    lane128 = lax.broadcasted_iota(jnp.int32, (1, 128), 1)
    slot_rows = jnp.where(lane128 == 0, patch, jnp.where(lane128 == 1, valid, 0.0)).T
    row128 = lax.broadcasted_iota(jnp.int32, (128, 256), 0)
    meta = jnp.where(row128 == 0, ids_t[0:1, :].astype(F32), 0.0)
    meta = jnp.where(row128 == 1, ids_t[1:2, :].astype(F32), meta)
    meta = jnp.where(row128 == 2, gates_t[0:1, :].astype(F32), meta)
    meta = jnp.where(row128 == 3, gates_t[1:2, :].astype(F32), meta).T
    token = lax.broadcasted_iota(jnp.int32, (PATCHES, 256), 0)
    holds = token == slot_rows[0:1, :].astype(jnp.int32)
    slot_lane = lax.broadcasted_iota(jnp.int32, (1, 256), 1)
    slot_expert = (slot_lane >> 3).astype(F32)
    usable = (slot_lane & 7).astype(F32) < slot_rows[1:2, :]
    gate = jnp.where(meta[:, 0:1] == slot_expert, meta[:, 2:3], 0.0)
    gate += jnp.where(meta[:, 1:2] == slot_expert, meta[:, 3:4], 0.0)
    placing = jnp.where(holds & usable, gate, 0.0).astype(BF16)
    choosing = jnp.where(holds, 1.0, 0.0).astype(BF16)

    acc[...] = jnp.zeros_like(acc)
    pl.semaphore_wait(barrier, len(near))

    def ring(half, stage, sign):
        along_z = (half == 0) == (stage == 1)
        return zdev(sign + NZ) if along_z else ydev(sign + NY)

    def first_copy(half, slot):
        source = 0 if slot < 3 else slot - 2
        if half == 0:
            src, dst = wg0.at[source, y, c], wg0.at[slot, y, c]
        else:
            src, dst = wg1.at[z, source, c], wg1.at[z, slot, c]
        return remote(
            src, dst, s1_send.at[half], s1_recv.at[half, slot - 1], ring(half, 1, -1 if slot % 2 else 1)
        )

    def chunk_ref(half, pos, k):
        low, high = CHUNKS[k]
        if half == 0:
            return wg0.at[low:high, pos % NY, c]
        return wg1.at[pos % NZ, low:high, c]

    def here(half):
        return y if half == 0 else z

    def ring_copy(half, way, step, k):
        pos = here(half) - (step - 1) if way == 0 else here(half) + (step - 1)
        piece = chunk_ref(half, pos + 8, k)
        index = (step - 1) * 5 + k
        return remote(
            piece, piece, ring_send.at[half], ring_recv.at[half, way, index], ring(half, 2, 1 if way == 0 else -1)
        )

    def core_copy_w(half, pos, k):
        piece = chunk_ref(half, pos + 8, k)
        return remote(piece, piece, core_send.at[half], core_recv.at[half, k], core)

    def share(half, pos, k):
        core_copy_w(half, pos, k).start()

    started = []

    def go(copy):
        copy.start()
        started.append(copy)

    def begin(k):
        for half in range(2):
            for way in range(2):
                ring_copy(half, way, 1, k).start()
        for half in range(2):
            share(half, here(half), k)

    def last_way(k):
        return 1 if k in (1, 2) else 0

    def advance(way, step, k):
        for half in range(2):
            ring_copy(half, way, step, k).wait_recv()
            if step < 3 or (step == 3 and way == last_way(k)):
                ring_copy(half, way, step + 1, k).start()
            share(half, here(half) - step if way == 0 else here(half) + step, k)

    col = lax.broadcasted_iota(jnp.int32, (1, 256), 1)
    inner = col & (ROWS - 1)
    own_slot = col >> 5
    absolute = jnp.where(inner < STRIP, STRIP * (col >> 4) + inner, -4096)
    turned = ((y + NY + slot_offset(own_slot)) % NY) * 2 + ((col >> 4) & 1)
    relative = jnp.where(inner < STRIP, STRIP * turned + inner, -4096)

    def strip_pick(first, count, target):
        feature = lax.broadcasted_iota(jnp.int32, (count, 256), 0) + first
        return jnp.where(feature == target, 1.0, 0.0).astype(BF16)

    def expand(m):
        low = (208 * m) // 128 * 128
        wide = min(384, D - low)
        exp0[m] = dot(normed[:, low : low + wide], strip_pick(low - 208 * m, wide, absolute)).astype(BF16)
        exp1[m] = dot(normed[:, low : low + wide], strip_pick(low - 208 * m, wide, relative)).astype(BF16)

    def project(k):
        acc[:, 0:CUT] += dot(exp0[(z + NZ + OFFSETS[k]) % NZ], wg0[k].reshape(256, CUT))

    def finish(k):
        low, high = CHUNKS[k]
        for half, piece in enumerate((wg0.at[low:high, :, c], wg1.at[:, low:high, c])):
            remote(piece, piece, core_send.at[half], core_recv.at[half, k], core).wait_recv()
        for slot in range(*CHUNKS[k]):
            project(slot)

    for half in range(2):
        first_copy(half, 1).start()
        first_copy(half, 2).start()
    for at, entry in enumerate(ROUTE):
        if entry[0] == "start":
            begin(entry[1])
        elif entry[0] == "first":
            for half in range(2):
                first_copy(half, entry[1]).wait_recv()
                if entry[1] <= 5:
                    first_copy(half, entry[1] + 2).start()
        else:
            advance(*entry)
        if at == 0:
            for load in loads[6:9]:
                load.wait()
            values = images[...].astype(F32)
            image_mean = jnp.mean(values, axis=-1, keepdims=True)
            center = values - image_mean
            spread = jnp.mean(center * center, axis=-1, keepdims=True)
            normed = (center * lax.rsqrt(spread + 1e-06) * attn_gain[...].reshape(1, D)).astype(BF16)
        if 8 <= at < 24 and at % 2 == 0:
            expand((at - 8) // 2)
    for k in range(5):
        finish(k)
    for k in range(8):
        part = dot(exp1[k], wg1[k].reshape(256, D - CUT)[:, 0 : 1280 - CUT])
        late = part if k == 0 else late + part
    acc[:, CUT:1280] = late
    lane = lax.broadcasted_iota(jnp.int32, (1, QP), 1)
    keys = acc[:, 384:896].astype(BF16).astype(F32)
    keys = jnp.where((lane >= 32) & (lane < 448), keys, 0.0).T.astype(BF16)
    vals = acc[:, 768:1280].astype(BF16).astype(F32)

    def sum_copy(h, d):
        return remote(
            summed.at[128 * h : 128 * h + 128, quarter((x + d) % NX)], landed.at[h, d - 1, :, 0:QW],
            x_send.at[h, d - 1], x_recv.at[h, d - 1], xdev(d),
        )

    def tail_copy(h, d):
        return remote(
            summed.at[128 * h : 128 * h + 128, 4 * QW : D], landed.at[h, d - 1, :, QW:QP],
            t_send.at[h, d - 1], t_recv.at[h, d - 1], xdev(d),
        )

    for half_rows in range(2):
        low = 128 * half_rows
        query = pltpu.roll(acc[low : low + 128, 0:512].astype(BF16).astype(F32), 32, 1)
        mixed = jnp.zeros((128, QP), F32)
        for h in range(HEADS_HERE):
            in_q = (lane >= 32 + HEAD_DIM * h) & (lane < 32 + HEAD_DIM * (h + 1))
            in_v = (lane >= 64 + HEAD_DIM * h) & (lane < 64 + HEAD_DIM * (h + 1))
            scores = dot(jnp.where(in_q, query, 0.0).astype(BF16), keys) * HEAD_DIM ** (-0.5)
            top = jnp.max(scores, axis=-1, keepdims=True)
            grown = jnp.exp(scores - top)
            probs = (grown / jnp.sum(grown, axis=-1, keepdims=True)).astype(BF16)
            mixed += dot(probs, jnp.where(in_v, vals, 0.0).astype(BF16))
        heads = pltpu.roll(mixed.astype(BF16).astype(F32), 32, 1)
        heads = jnp.where(lane >= 96, heads, 0.0).T.astype(BF16)

        def spread_out(k, carry, low=low, heads=heads):
            weights = wg1[k].reshape(256, D - CUT)[:, 1152 - CUT : D - CUT]
            outp[k, :, low : low + 128] = dot(weights, heads).astype(BF16)
            return carry

        lax.fori_loop(0, 8, spread_out, 0)
        for t in range(13):
            total = None
            for m in range(128 * t // 208, (128 * t + 127) // 208 + 1):
                term = dot(strip_pick(128 * t - 208 * m, 128, relative), outp[m, :, low : low + 128])
                total = term if total is None else total + term
            summed[low : low + 128, 128 * t : 128 * t + 128] = total.T.astype(BF16)
        for d in (2, 1, 3):
            go(sum_copy(half_rows, d))
            pl.when((x + d) % NX == 0)(tail_copy(half_rows, d).start)

    real = (lane < QW) | tail
    own = jnp.concatenate([summed[:, quarter(x)], summed[:, 4 * QW : D]], axis=1).astype(F32)
    base = jnp.concatenate([images[:, quarter(x)], images[:, 4 * QW : D]], axis=1).astype(F32)
    for h in range(2):
        for d in (1, 3, 2):
            sum_copy(h, d).wait_recv()
            pl.when(tail)(tail_copy(h, d).wait_recv)

    attn = own
    for d in (1, 2, 3):
        attn += jnp.concatenate([landed[0, d - 1], landed[1, d - 1]], axis=0).astype(F32)
    residual = jnp.where(real, base + attn, 0.0)

    routed = jnp.where(real, residual - image_mean, 0.0).astype(BF16)
    chosen = dot(choosing, routed, ((0,), (0,)))

    def folded(value):
        return jnp.concatenate([value[:, 0:256].reshape(32, 8, 256), value[:, 256:512].reshape(32, 8, 256)], axis=1).astype(BF16)

    def unfolded(value):
        value = value.reshape(32, 16, 256).astype(F32)
        return value[:, 0:8].reshape(256, 256).astype(BF16), value[:, 8:16].reshape(256, 256).astype(BF16)

    picked[...] = folded(chosen)

    def a_copy(i, d):
        to_y, to_z = (y + 2 * i) % NY, (z + d) % NZ
        return remote(
            picked.at[4 * to_z + to_y // 2], arrived.at[pair, z], a_send, a_recv, device(x, to_y, to_z, c)
        )

    for i, d in FAR:
        a_copy(i, d).start()
    arrived[pair, z] = picked[4 * z + pair]

    class Both:
        def __init__(self, main, extra, is_tail):
            self.main, self.extra, self.is_tail = main, extra, is_tail

        def start(self):
            self.main.start()
            pl.when(self.is_tail)(self.extra.start)

        def wait_send(self):
            self.main.wait_send()
            pl.when(self.is_tail)(self.extra.wait_send)

        def wait_recv(self):
            self.main.wait_recv()
            pl.when(self.is_tail)(self.extra.wait_recv)

    def pieces(src_main, dst_main, src_extra, dst_extra, send, recv, target, is_tail):
        return Both(
            remote(src_main, dst_main, send.at[0], recv.at[0], target),
            remote(src_extra, dst_extra, send.at[1], recv.at[1], target),
            is_tail,
        )

    def all_of(send, recv):
        return remote(picked.at[0:31], home.at[0:31], send, recv, core)

    all_of(a_send, a_recv).wait_recv()
    left, right = unfolded(arrived[...])
    rows[par, c, :, quarter(x)] = jnp.concatenate([left, right[:, 0:128]], axis=1)

    @pl.when(tail)
    def _():
        rows[par, c, :, 4 * QW : D] = right[:, 128:256]

    def same(parity, q_index, low, high, send, recv, target):
        main = rows.at[parity, c, low:high, quarter(q_index)]
        extra = rows.at[parity, c, low:high, 4 * QW : D]
        return pieces(main, main, extra, extra, send, recv, target, q_index == 0)

    def cut(which, j):
        return ((0, 128), (128, 256))[j] if which == 0 else ((0, 64), (64, 128))[j]

    def x_piece(which, way, j, q_index):
        low, high = cut(which, way if j == 2 else j)
        return same(
            par if which == 0 else 1 - par, q_index, low, high,
            xg_send.at[which, way, j], xg_recv.at[which, way, j], xdev(1 if way == 0 else 3),
        )

    def x_from(way, j):
        hops = 2 if j == 2 else 1
        return (x + NX - hops) % NX if way == 0 else (x + hops) % NX

    def y_piece(j, parity):
        low, high = (0, 128) if j == 0 else (128, 256)
        q_index = (x + (0, 0, NX - 1, 1, 2)[j]) % NX
        return same(parity, q_index, low, high, yp_send.at[j], yp_recv.at[j], mate)

    group_sent = []

    def to_core_all(main, extra, which):
        return pieces(main, main, extra, extra, cg_send, cg_recv.at[which], core, x >= 0)


    def put(copy):
        copy.start()
        group_sent.append(copy)

    def over(which, q_index, low, high):
        same(par if which == 0 else 1 - par, q_index, low, high, cg_send, cg_recv.at[which], core).start()

    def take_x(which, way, j):
        q_index = x_from(way, j)
        x_piece(which, way, j, q_index).wait_recv()
        if j == way:
            put(x_piece(which, way, 2, q_index))
        if which == 0 and (way, j) in ((0, 1), (1, 1), (1, 2)):
            put(y_piece({(0, 1): 2, (1, 1): 3, (1, 2): 4}[way, j], par))
        over(which, q_index, *cut(which, way if j == 2 else j))

    def send_x(which):
        for way, j in ((0, 0), (1, 1), (0, 1), (1, 0)):
            put(x_piece(which, way, j, x))

    def take_y(j):
        y_piece(j, 1 - par).wait_recv()
        if j == 0:
            send_x(1)
        over(1, (x + (0, 0, NX - 1, 1, 2)[j]) % NX, *((0, 128) if j == 0 else (128, 256)))

    send_x(0)
    put(y_piece(0, par))
    put(y_piece(1, par))
    over(0, x, 0, 256)

    def expert(parity, core_index):
        values = rows[parity, core_index].astype(F32)
        center = values - jnp.mean(values, axis=-1, keepdims=True)
        spread = jnp.mean(center * center, axis=-1, keepdims=True)
        normed = (center * lax.rsqrt(spread + 1e-06) * mlp_gain[...].reshape(1, D)).astype(BF16)
        hidden = gelu_tanh(dot(normed, w_in[...])).astype(BF16)
        parts[parity, core_index] = dot(hidden, w_out[...]).astype(BF16)

    def r1_copy(k):
        parity = par if k == 0 else 1 - par
        return remote(parts.at[parity, 1 - c], r1.at[parity], r1_send.at[k], r1_recv.at[k], core)

    take_x(0, 0, 0)
    take_x(0, 1, 1)
    take_y(0)
    take_x(0, 0, 1)
    take_x(0, 1, 0)
    take_y(1)
    take_x(0, 0, 2)
    take_x(0, 1, 2)
    take_x(1, 0, 0)
    take_x(1, 1, 1)
    for load in loads[9:]:
        load.wait()
    to_core_all(rows.at[:, :, :, 0:QW], rows.at[0, 0, :, 0:128], 0).wait_recv()
    expert(par, 1 - c)
    r1_copy(0).start()
    take_x(1, 0, 1)
    take_x(1, 1, 0)
    take_y(3)
    take_y(2)
    expert(par, c)
    take_x(1, 0, 2)
    take_x(1, 1, 2)
    take_y(4)
    def both_cores(parity):
        q[parity] = (parts[parity, c].astype(F32) + r1[parity].astype(F32)).astype(BF16)

    def quarters(src, rows_of, rows_to, dst, send, recv, d):
        to = (x + d) % NX
        return pieces(
            src.at[rows_of, quarter(to)], dst.at[d - 1, rows_to, 0:QW], src.at[rows_of, 4 * QW : D], dst.at[d - 1, rows_to, QW:QP],
            send.at[d - 1], recv.at[d - 1], xdev(d), to == 0,
        )

    def got(copy):
        copy.main.wait_recv()
        pl.when(tail)(copy.extra.wait_recv)

    def own_sum_copy(d):
        return quarters(q.at[par], pl.ds(0, FIRST), pl.ds(0, FIRST), r2a, r2_send, r2_recv, d)

    def mate_sum_copy(i, d):
        part = pl.ds(i * HALF, HALF)
        return quarters(q.at[1 - par], part, part, r2c, r2c_send.at[i], r2c_recv.at[i], d)

    def rest_copy():
        return remote(q.at[1 - par, FIRST:256], r2b, r2y_send, r2y_recv, mate)

    def late_copy(d):
        return quarters(sb, pl.ds(0, 256 - FIRST), pl.ds(0, 256 - FIRST), r3b, r3_send, r3_recv, d)

    def summed_copy(i):
        part = pl.ds(i * HALF, HALF)
        return remote(sa.at[part], r3a.at[part], r3y_send.at[i], r3y_recv.at[i], mate)

    def mine_of(value):
        return jnp.concatenate([value[:, quarter(x)], value[:, 4 * QW : D]], axis=1).astype(F32)

    r1_copy(0).wait_recv()
    both_cores(par)
    for d in (2, 1, 3):
        own_sum_copy(d).start()
    to_core_all(rows.at[:, :, :, 0:QW], rows.at[0, 0, :, 0:128], 1).wait_recv()
    expert(1 - par, 1 - c)
    r1_copy(1).start()
    expert(1 - par, c)
    r1_copy(1).wait_recv()
    both_cores(1 - par)
    rest_copy().start()
    for i in range(2):
        for d in (2, 1, 3):
            mate_sum_copy(i, d).start()
    for d in (1, 3, 2):
        got(own_sum_copy(d))
    own_total = mine_of(q.at[par, 0:FIRST])
    for d in (1, 2, 3):
        own_total += r2a[d - 1].astype(F32)

    def pass_on(i):
        for d in (1, 3, 2):
            got(mate_sum_copy(i, d))
        low, high = i * HALF, (i + 1) * HALF
        total = mine_of(q.at[1 - par, low:high])
        for d in (1, 2, 3):
            total += r2c[d - 1, low:high].astype(F32)
        sa[low:high] = jnp.where(real, total, 0.0).astype(BF16)
        summed_copy(i).start()

    pass_on(0)
    rest_copy().wait_recv()
    sb[...] = (q[par, FIRST:256].astype(F32) + r2b[...].astype(F32)).astype(BF16)
    for d in (2, 1, 3):
        late_copy(d).start()
    pass_on(1)
    total = mine_of(sb)
    summed_copy(0).wait_recv()
    summed_copy(1).wait_recv()
    high_rows = jnp.where(real, own_total + r3a[...].astype(F32), 0.0)
    for d in (1, 3, 2):
        got(late_copy(d))
        total += r3b[d - 1].astype(F32)
    result = jnp.concatenate([high_rows, jnp.where(real, total, 0.0)], axis=0)

    returning[...] = folded(result).reshape(4, 8, 16, 256)

    def aa_copy(i, d):
        to_y, to_z = (y + 2 * i) % NY, (z + d) % NZ
        return remote(
            returning.at[to_y // 2, to_z], home.at[4 * z + pair], aa_send, aa_recv, device(x, to_y, to_z, c)
        )

    for i, d in FAR:
        aa_copy(i, d).start()
    home[4 * z + pair] = returning[pair, z]
    all_of(aa_send, aa_recv).wait_recv()
    left, right = unfolded(home[...])
    final[...] = (residual + jnp.concatenate([dot(placing, left), dot(placing, right)], axis=1)).astype(BF16)

    def f_copy(d):
        to = pl.ds(pl.multiple_of((x + d) % NX * 64, 64), 64)
        return pieces(
            final.at[to, 0:QW], gathered.at[:, quarter(x)],
            final.at[to, QW:QP], gathered.at[:, 4 * QW : D],
            f_send.at[d - 1], f_recv.at[d - 1], xdev(d), tail,
        )

    for d in (2, 1, 3):
        f_copy(d).start()
    mine = pl.ds(pl.multiple_of(x * 64, 64), 64)
    gathered[:, quarter(x)] = final[mine, 0:QW]

    @pl.when(tail)
    def _():
        gathered[:, 4 * QW : D] = final[mine, QW:QP]

    for d in (1, 3, 2):
        copy = f_copy(d)
        copy.main.wait_recv()
        pl.when((x + NX - d) % NX == 0)(copy.extra.wait_recv)
    out[...] = gathered[...]

    for copy in started:
        copy.wait_send()
    for h in range(2):
        for d in (1, 2, 3):
            pl.when((x + d) % NX == 0)(tail_copy(h, d).wait_send)
    all_of(a_send, a_recv).wait_send()
    all_of(aa_send, aa_recv).wait_send()
    for half, (strips, ringed, shared) in enumerate(
        ((wg0.at[0:7, 0, 0], wg0.at[:, 0:7, 0], wg0.at[:, :, 0]), (wg1.at[0, 0:7, 0], wg1.at[0:7, :, 0], wg1.at[:, :, 0]))
    ):
        remote(strips, strips, s1_send.at[half], s1_recv.at[half, 0], core).wait_send()
        remote(ringed, ringed, ring_send.at[half], ring_recv.at[half, 0, 0], core).wait_send()
        remote(shared, shared, core_send.at[half], core_recv.at[half, 0], core).wait_send()
    to_core_all(rows.at[:, :, :, 0 : 2 * QW], rows.at[0, :, :, 0:128], 0).wait_send()
    for copy in group_sent:
        copy.wait_send()
    for k in range(2):
        r1_copy(k).wait_send()
    for d in (1, 2, 3):
        own_sum_copy(d).wait_send()
        mate_sum_copy(0, d).wait_send()
        mate_sum_copy(1, d).wait_send()
        late_copy(d).wait_send()
        f_copy(d).wait_send()
    rest_copy().wait_send()
    summed_copy(0).wait_send()
    summed_copy(1).wait_send()


def block(images, attn_gain, mlp_gain, qkv, proj_t, ids_t, gates_t, kept, counts, w_in, w_out):
    sem = pltpu.SemaphoreType.DMA
    vm = pl.BlockSpec(memory_space=pltpu.VMEM)
    hbm = pl.BlockSpec(memory_space=pl.ANY)

    def v(*shape, kind=BF16):
        return pltpu.VMEM(shape, kind)

    return pl.pallas_call(
        block_kernel,
        name="block",
        out_shape=jax.ShapeDtypeStruct((64, D), BF16),
        in_specs=[hbm] * 11,
        out_specs=vm,
        scratch_shapes=[
            v(PATCHES, D), v(D, kind=F32), v(D, kind=F32), v(3, STRIP, 416), v(STRIP, 416),
            v(2, PATCHES, kind=jnp.int32), v(2, PATCHES), v(8, EXPERTS, kind=jnp.int32), v(1, EXPERTS, kind=jnp.int32),
            v(8, NY, 2, ROWS, CUT), v(NZ, 8, 2, ROWS, D - CUT), v(4, ROWS, D, kind=F32),
            v(8, PATCHES, 256), v(8, PATCHES, 256), v(PATCHES, 1280, kind=F32), v(8, PATCHES, 256), v(PATCHES, D),
            v(2, 3, 128, QP),
            v(D, 512), v(512, D), v(32, 16, 256), v(4, 8, 16, 256), v(2, 2, 256, D), v(2, 2, 256, D), v(2, 256, D),
            v(2, 256, D), v(3, FIRST, QP), v(3, FIRST, QP), v(256 - FIRST, D), v(FIRST, QP), v(256 - FIRST, D), v(FIRST, QP), v(3, 256 - FIRST, QP),
            v(4, 8, 16, 256), v(32, 16, 256), v(256, QP), v(64, D),
            sem((2,)), sem((2, 7)), sem((2,)), sem((2, 2, 20)), sem((2,)), sem((2, 5)),
            sem((2, 3)), sem((2, 3)), sem((2, 3)), sem((2, 3)),
            sem((11,)), sem, sem, sem((5, 2)), sem((5, 2)),
            sem((2, 2, 3, 2)), sem((2, 2, 3, 2)), sem((2,)), sem((2, 2)),
            sem((2,)), sem((2,)), sem((3, 2)), sem((3, 2)), sem((2, 3, 2)), sem((2, 3, 2)), sem, sem, sem((3, 2)), sem((3, 2)), sem((2,)), sem((2,)),
            sem, sem, sem((3, 2)), sem((3, 2)),
        ],
        compiler_params=pltpu.CompilerParams(collective_id=1, has_side_effects=True, vmem_limit_bytes=56 << 20),
    )(images, attn_gain, mlp_gain, qkv, proj_t, ids_t, gates_t, kept, counts, w_in, w_out)


def on_device(
    images, attn_gain, qkv_weight, proj_weight, mlp_gain, expert_in, expert_out,
    gate_values, expert_ids, kept_patches, kept_counts,
):
    return block(
        images, attn_gain, mlp_gain, qkv_weight, proj_weight.T, expert_ids.T, gate_values.T,
        kept_patches[0].T, kept_counts, expert_in, expert_out,
    )


def solution(mesh):
    placed = (
        P("dp", None), P(), P(None, "dp", "mp"), P("mp", "dp"), P(), P(None, ("dp", "mp")), P(("dp", "mp"), None),
        P("dp", None), P("dp", None), P("dp", None, None), P("dp", None),
    )
    return jax.shard_map(on_device, mesh=mesh, in_specs=placed, out_specs=P(("dp", "mp"), None), check_vma=False)
```
